128 devices in a mesh: gx: 16 (over z, y), yz: 8 (over x, core).
Axes of the slice: x: 4, y: 4, z: 4, core: 2. Of those that a mesh axis runs over, the one named last changes fastest.
Arguments:
- field: float32 [512, 512, 1024], P('gx', None, 'yz'), may hold values from -58 to 58, as said below
- start: float32 [512, 128], replicated, may hold values from -6 to 6
Outputs:
- basis: float32 [512, 128], replicated
- gram_y: float32 [1024, 1024], P('yz', 'gx')
The draws below stay inside these ranges and needn't reach their ends.
Inputs may be any that keep to these rules, and one draw needn't show every extreme that they name: `field`: every cell is a real number at most a few tens in magnitude.
All inputs are finite; a program needn't handle non-finite values.
Results may differ from the reference program's by a relative error of at most 0.00025.
Values sent between devices are 32-bit elements; how exact they have to be, the bound alone decides.
A program may use at most 128 MiB of HBM per device.

```python
import math
import jax
import jax.numpy as jnp
from jax import lax

NX = 512
NY = 1024
RANK = 128
NZ = 512
ITERS = 4


def draw_field(key, part):
    key = jax.random.fold_in(key, 11)
    first, second, third = jax.random.split(key, 3)
    noise = jnp.clip(jax.random.normal(first, (NX, NZ, NY), jnp.float32), -6.0, 6.0)
    row_scale = jnp.exp(jax.random.uniform(second, (NX, 1, 1), jnp.float32, 0.0, math.log(3.0)))
    fibre_scale = jnp.exp(jax.random.uniform(third, (1, NZ, NY), jnp.float32, 0.0, math.log(2.0)))
    mixed = noise + 0.6 * jnp.roll(noise, 1, axis=0)
    return row_scale * fibre_scale * mixed


def centred(key, shape, spread, limit, dtype=jnp.bfloat16):
    values = jax.random.normal(key, shape, jnp.float32) * spread
    return jnp.minimum(jnp.maximum(values, -limit), limit).astype(dtype)


def setup_inputs(seed: int = 0) -> dict:
    streams_of = jax.random.split(jax.random.key(seed), 3)
    return {
        "field": draw_field(jax.random.fold_in(streams_of[2], 71), 0),
        "start": centred(streams_of[1], (NX, RANK), 1.0, 6.0, jnp.float32),
    }


def orthonormal(product):
    cross = jnp.dot(product.T.astype(jnp.float32), product.astype(jnp.float32), precision=lax.Precision.HIGHEST, preferred_element_type=jnp.float32)
    lower = lax.linalg.cholesky(cross)
    return lax.linalg.triangular_solve(lower, product, left_side=False, lower=True, transpose_a=True)

def reference(field, start):
    flat = field.reshape(NX, NZ * NY)
    gram_x = jnp.dot(flat.astype(jnp.float32), flat.T.astype(jnp.float32), precision=lax.Precision.HIGHEST, preferred_element_type=jnp.float32) / (NY * NZ)
    basis = start
    for step in range(ITERS):
        basis = orthonormal(jnp.dot(gram_x.astype(jnp.float32), basis.astype(jnp.float32), precision=lax.Precision.HIGHEST, preferred_element_type=jnp.float32))
    core = jnp.dot(basis.T.astype(jnp.float32), flat.astype(jnp.float32), precision=lax.Precision.HIGHEST, preferred_element_type=jnp.float32)
    core = core.reshape(RANK * NZ, NY)
    gram_y = jnp.dot(core.T.astype(jnp.float32), core.astype(jnp.float32), precision=lax.Precision.HIGHEST, preferred_element_type=jnp.float32) / (RANK * NZ)
    return (basis, gram_y)
```

```python
import functools

import jax
import jax.numpy as jnp
from jax import lax
from jax.experimental import pallas as pl
from jax.experimental.pallas import tpu as pltpu
from jax.sharding import PartitionSpec as P

ITERS = 4
ROUNDS = 4
RANK = 128
STRIP = 32
F32 = jnp.float32
BF16 = jnp.bfloat16
MESH = pl.DeviceIdType.MESH
NN = (((1,), (0,)), ((), ()))
NT = (((1,), (1,)), ((), ()))
TN = (((0,), (0,)), ((), ()))


def dot(left, right, dims, precision=None):
    return lax.dot_general(left, right, dims, precision=precision, preferred_element_type=F32)


def dot_exact(left, right, dims):
    return dot(left, right, dims, lax.Precision.HIGHEST)


def split(value):
    high = value.astype(BF16)
    return high, (value - high.astype(F32)).astype(BF16)


def split3(value):
    high = value.astype(BF16)
    rest = value - high.astype(F32)
    return (high,) + split(rest)


def position():
    gx, yz = lax.axis_index("gx"), lax.axis_index("yz")
    return gx, yz, gx // 4, gx % 4, yz // 2, yz % 2


def chip_of_step(step):
    gx, yz, z, y, x, c = position()
    sign = 1 + 2 * c
    i, a, b = step % 4, step // 4 % 4, step // 16
    to_z, to_y, to_x = (z + sign * i) % 4, (y + sign * (a + i)) % 4, (x + sign * (b + i)) % 4
    return to_z * 4 + to_y, to_x


def device_of_step(step):
    c = lax.axis_index("yz") % 2
    step = (step + 64 * c) % 128
    to_gx, to_x = chip_of_step(step % 4 + step // 8 * 4)
    return to_gx, to_x * 2 + (c + step // 4) % 2


def each_other_device(action):
    gx, yz = lax.axis_index("gx"), lax.axis_index("yz")

    def body(step, carry):
        to_gx, to_yz = device_of_step(step)

        @pl.when((to_gx != gx) | (to_yz != yz))
        def _():
            action(to_gx, to_yz)

        return carry

    lax.fori_loop(0, 128, body, 0)


def each_other_chip(action):
    c = lax.axis_index("yz") % 2

    def body(step, carry):
        to_gx, to_x = chip_of_step(step)
        action(to_gx, to_x, to_x * 2 + c)
        return carry

    lax.fori_loop(1, 64, body, 0)


def meet_all():
    barrier = pltpu.get_barrier_semaphore()
    each_other_device(
        lambda to_gx, to_yz: pl.semaphore_signal(
            barrier, inc=1, device_id=(to_gx, to_yz), device_id_type=MESH
        )
    )
    pl.semaphore_wait(barrier, 127)


def send_to(src, dst, send_sem, recv_sem, to_gx, to_yz):
    pltpu.make_async_remote_copy(
        src_ref=src,
        dst_ref=dst,
        send_sem=send_sem,
        recv_sem=recv_sem,
        device_id=(to_gx, to_yz),
        device_id_type=MESH,
    ).start()


def wait_for(ref, sem):
    pltpu.make_async_copy(ref, ref, sem).wait()


def reciprocal(value):
    guess = pltpu.reciprocal(value, approx=True)
    guess = guess * (2.0 - value * guess)
    return guess * (2.0 - value * guess)


def inverse_factor(cross):
    n = RANK
    row = lax.broadcasted_iota(jnp.int32, (n, n), 0)
    col = lax.broadcasted_iota(jnp.int32, (n, n), 1)
    eye = row == col
    diagonal = jnp.where(eye, cross, 0.0)
    scale_row = lax.rsqrt(jnp.sum(diagonal, axis=0, keepdims=True))
    scale_col = lax.rsqrt(jnp.sum(diagonal, axis=1, keepdims=True))
    a = cross * scale_row * scale_col
    e = jnp.where(eye, 1.0, 0.0)
    local = lax.broadcasted_iota(jnp.int32, (STRIP, n), 0)
    done = []
    for strip in range(n // STRIP):
        ra = a[STRIP * strip : STRIP * (strip + 1)]
        re = e[STRIP * strip : STRIP * (strip + 1)]
        alpha = jnp.zeros((STRIP, n), F32)
        beta = jnp.zeros((STRIP, n), F32)
        for panel in range(STRIP // 8):
            base = STRIP * strip + 8 * panel
            c = [jnp.broadcast_to(ra[:, base + j : base + j + 1], (STRIP, n)) for j in range(8)]
            for pair in range(4):
                k = 8 * panel + 2 * pair
                c0, c1 = c[2 * pair], c[2 * pair + 1]
                p00, p01, p11 = c0[k : k + 1], c1[k : k + 1], c1[k + 1 : k + 2]
                det = p00 * p11 - p01 * p01
                inv = reciprocal(det)
                below = local > k + 1
                m0 = jnp.where(below, (c0 * p11 - c1 * p01) * inv, 0.0)
                m1 = jnp.where(below, (c1 * p00 - c0 * p01) * inv, 0.0)
                for j in range(2 * pair + 2, 8):
                    c[j] = c[j] - m0 * c[j][k : k + 1] - m1 * c[j][k + 1 : k + 2]
                if k + 2 < STRIP:
                    ra = ra - m0 * ra[k : k + 1] - m1 * ra[k + 1 : k + 2]
                    re = re - m0 * re[k : k + 1] - m1 * re[k + 1 : k + 2]
                s0 = lax.rsqrt(p00)
                s1 = lax.rsqrt(det * (s0 * s0))
                alpha = jnp.where(local == k, s0, jnp.where(local == k + 1, s1, alpha))
                beta = jnp.where(local == k + 1, p01 * (s0 * s0), beta)
        ua = alpha * (ra - beta * pltpu.roll(ra, 1, 0))
        ue = alpha * (re - beta * pltpu.roll(re, 1, 0))
        done.append(ue)
        if strip + 1 < n // STRIP:
            h, m, l = split3(jnp.concatenate([ua, ue], axis=1))
            left = jnp.concatenate([part[:, :n] for part in (h, h, m, h, m, l)], axis=0)
            right = jnp.concatenate([h, m, h, l, m, h], axis=0)
            update = dot(left, right, TN)
            a = a - update[:, :n]
            e = e - update[:, n:]
    return jnp.concatenate(done, axis=0) * scale_row


def kernel(
    field, start, basis, gram_y,
    landed, high, low, both, cross,
    half_gram, pair_gram, sum_gram, parts_gram, all_gram, gram_x,
    core_high, core_low, give, keep, pair_y, parts_y,
    field_send, field_recv, gram_send, gram_recv, y_send, y_recv,
):
    gx, yz, z, y, x, c = position()
    chip = gx * 4 + x
    meet_all()

    own = pl.ds(pl.multiple_of(yz * 512 + gx * 32, 32), 32)
    for r in range(ROUNDS):
        pltpu.make_async_copy(
            field.at[:, (gx * 8 + yz) * ROUNDS + r], landed.at[r, own], field_recv.at[r]
        ).start()
        each_other_device(
            lambda to_gx, to_yz, r=r: send_to(
                field.at[:, (to_gx * 8 + to_yz) * ROUNDS + r],
                landed.at[r, own],
                field_send.at[r],
                field_recv.at[r],
                to_gx,
                to_yz,
            )
        )

    for r in range(ROUNDS):
        wait_for(landed.at[r], field_recv.at[r])
        for j in range(8):
            h, l = split(landed[r, 512 * j : 512 * (j + 1), :])
            high[r, :, 128 * j : 128 * (j + 1)] = h
            low[r, :, 128 * j : 128 * (j + 1)] = l
        h, l = high[r], low[r]
        if r == 0:
            both[...] = dot(h, h, NT)
            cross[...] = dot(h, l, NT)
        else:
            both[...] += dot(h, h, NT)
            cross[...] += dot(h, l, NT)
    for j in range(4):
        columns = slice(128 * j, 128 * (j + 1))
        half_gram[512 * j : 512 * (j + 1), :] = 0.5 * both[:, columns] + cross[:, columns]

    mine = pl.ds(pl.multiple_of(c * 1024, 1024), 1024)
    other = pl.ds(pl.multiple_of((1 - c) * 1024, 1024), 1024)
    partner = x * 2 + 1 - c
    send_to(half_gram.at[other], pair_gram, gram_send.at[0], gram_recv.at[0], gx, partner)
    wait_for(pair_gram, gram_recv.at[0])
    sum_gram[...] = half_gram[mine, :] + pair_gram[...]
    each_other_chip(
        lambda to_gx, to_x, to_yz: send_to(
            sum_gram.at[pl.ds(pl.multiple_of((to_gx * 4 + to_x) * 16, 16), 16)],
            parts_gram.at[chip],
            gram_send.at[1],
            gram_recv.at[1],
            to_gx,
            to_yz,
        )
    )
    parts_gram[chip] = sum_gram[pl.ds(pl.multiple_of(chip * 16, 16), 16), :]
    wait_for(parts_gram.at[pl.ds(0, 63)], gram_recv.at[1])
    piece = pl.ds(pl.multiple_of(c * 1024 + chip * 16, 16), 16)
    all_gram[piece, :] = jnp.sum(parts_gram[...], axis=0)
    each_other_chip(
        lambda to_gx, to_x, to_yz: send_to(
            all_gram.at[piece], all_gram.at[piece], gram_send.at[2], gram_recv.at[2], to_gx, to_yz
        )
    )
    wait_for(all_gram.at[pl.ds(0, 63 * 16)], gram_recv.at[2])
    send_to(all_gram.at[mine], all_gram.at[mine], gram_send.at[3], gram_recv.at[3], gx, partner)
    wait_for(all_gram.at[other], gram_recv.at[3])
    total = jnp.concatenate([all_gram[512 * j : 512 * (j + 1), :] for j in range(4)], axis=1)
    gram_x[...] = (total + total.T) * (1.0 / (512 * 1024))

    basis[...] = start[...]

    def iterate(step, carry):
        product = dot_exact(gram_x[...], basis[...], NN)
        basis[...] = dot_exact(product, inverse_factor(dot_exact(product, product, TN)), NT)
        return carry

    lax.fori_loop(0, ITERS, iterate, 0)

    b_high, b_low = split(basis[...].T)
    for r in range(ROUNDS):
        h, l = high[r], low[r]
        part = dot(b_high, h, NN) + (dot(b_high, l, NN) + dot(b_low, h, NN))
        core_high[RANK * r : RANK * (r + 1), :], core_low[RANK * r : RANK * (r + 1), :] = split(part)

    def columns_of(parity, j):
        at = pl.ds(pl.multiple_of((2 * j + parity) * 128, 128), 128)
        h, l = core_high[:, at], core_low[:, at]
        return dot(core_high[...], h, TN) + (dot(core_high[...], l, TN) + dot(core_low[...], h, TN))

    for j in range(4):
        give[j] = columns_of(1 - c, j)
        send_to(give.at[j], pair_y.at[j], y_send.at[j], y_recv.at[j], gx, partner)
    for j in range(4):
        keep[j] = columns_of(c, j)
    for j in range(4):
        wait_for(pair_y.at[j], y_recv.at[j])
        keep[j] = keep[j] + pair_y[j]

    def piece_y(to_gx, to_x):
        return keep.at[to_x, pl.ds(pl.multiple_of(to_gx * 64, 64), 64)]

    each_other_chip(
        lambda to_gx, to_x, to_yz: send_to(
            piece_y(to_gx, to_x), parts_y.at[chip], y_send.at[4], y_recv.at[4], to_gx, to_yz
        )
    )
    parts_y[chip] = piece_y(gx, x)[...]
    wait_for(parts_y.at[pl.ds(0, 63)], y_recv.at[4])
    gram_y[...] = (jnp.sum(parts_y[...], axis=0) * (1.0 / 65536)).T

    for r in range(ROUNDS):
        wait_for(landed.at[r, pl.ds(0, 127 * 32)], field_send.at[r])
    wait_for(pair_gram, gram_send.at[0])
    wait_for(parts_gram.at[pl.ds(0, 63)], gram_send.at[1])
    wait_for(parts_gram.at[pl.ds(0, 63)], gram_send.at[2])
    wait_for(all_gram.at[mine], gram_send.at[3])
    for j in range(4):
        wait_for(give.at[j], y_send.at[j])
    wait_for(parts_y.at[pl.ds(0, 63)], y_send.at[4])


def on_device(field, start):
    vmem = pl.BlockSpec(memory_space=pltpu.VMEM)
    return pl.pallas_call(
        kernel,
        out_shape=(
            jax.ShapeDtypeStruct((512, RANK), F32),
            jax.ShapeDtypeStruct((128, 64), F32),
        ),
        in_specs=[pl.BlockSpec(memory_space=pl.ANY), vmem],
        out_specs=(vmem, vmem),
        scratch_shapes=[
            pltpu.VMEM((ROUNDS, 4096, 128), F32),
            pltpu.VMEM((ROUNDS, 512, 1024), BF16),
            pltpu.VMEM((ROUNDS, 512, 1024), BF16),
            pltpu.VMEM((512, 512), F32),
            pltpu.VMEM((512, 512), F32),
            pltpu.VMEM((2048, 128), F32),
            pltpu.VMEM((1024, 128), F32),
            pltpu.VMEM((1024, 128), F32),
            pltpu.VMEM((64, 16, 128), F32),
            pltpu.VMEM((2048, 128), F32),
            pltpu.VMEM((512, 512), F32),
            pltpu.VMEM((512, 1024), BF16),
            pltpu.VMEM((512, 1024), BF16),
            pltpu.VMEM((4, 1024, 128), F32),
            pltpu.VMEM((4, 1024, 128), F32),
            pltpu.VMEM((4, 1024, 128), F32),
            pltpu.VMEM((64, 64, 128), F32),
            pltpu.SemaphoreType.DMA((ROUNDS,)),
            pltpu.SemaphoreType.DMA((ROUNDS,)),
            pltpu.SemaphoreType.DMA((4,)),
            pltpu.SemaphoreType.DMA((4,)),
            pltpu.SemaphoreType.DMA((5,)),
            pltpu.SemaphoreType.DMA((5,)),
        ],
        compiler_params=pltpu.CompilerParams(
            collective_id=0, has_side_effects=True, vmem_limit_bytes=56 << 20
        ),
    )(field, start)


def solution(mesh):
    placed = (P("gx", None, "yz"), P())
    return jax.shard_map(
        on_device, mesh=mesh, in_specs=placed, out_specs=(P(), P("yz", "gx")), check_vma=False
    )
```

```python
import functools

import jax
import jax.numpy as jnp
from jax import lax
from jax.experimental import pallas as pl
from jax.experimental.pallas import tpu as pltpu
from jax.sharding import PartitionSpec as P

ITERS = 4
ROUNDS = 4
RANK = 128
STRIP = 32
PANEL = 16
F32 = jnp.float32
BF16 = jnp.bfloat16
MESH = pl.DeviceIdType.MESH
NN = (((1,), (0,)), ((), ()))
NT = (((1,), (1,)), ((), ()))
TN = (((0,), (0,)), ((), ()))


def dot(left, right, dims, precision=None):
    return lax.dot_general(left, right, dims, precision=precision, preferred_element_type=F32)


def dot_exact(left, right, dims):
    return dot(left, right, dims, lax.Precision.HIGHEST)


def split(value):
    high = value.astype(BF16)
    return high, (value - high.astype(F32)).astype(BF16)


def split3(value):
    high = value.astype(BF16)
    rest = value - high.astype(F32)
    return (high,) + split(rest)


def position():
    gx, yz = lax.axis_index("gx"), lax.axis_index("yz")
    return gx, yz, gx // 4, gx % 4, yz // 2, yz % 2


def routes():
    gx, yz, z, y, x, c = position()
    sign = 1 + 2 * c
    to_z, to_y, to_x = ([(at + sign * i) % 4 for i in range(4)] for at in (z, y, x))
    return [[to_z[i] * 4 + to_y[j] for j in range(4)] for i in range(4)], to_x


CHIP_STEPS = [(i, (a + i) % 4, (b + i) % 4) for b in range(4) for a in range(4) for i in range(4)]


def each_other_device(action):
    to_gx, to_x = routes()
    c = lax.axis_index("yz") % 2
    to_x = [jnp.where(c == 0, to_x[i], to_x[(i + 2) % 4]) for i in range(4)]
    to_yz = [[2 * at + c for at in to_x], [2 * at + 1 - c for at in to_x]]
    for group in range(16):
        for flip in range(2):
            for i, j, k in CHIP_STEPS[4 * group : 4 * group + 4]:
                act = functools.partial(action, to_gx[i][j], to_yz[flip][k])
                if (i, j, k % 2, flip) == (0, 0, 0, 0):
                    pl.when(c != k // 2)(act)
                else:
                    act()


def each_other_chip(action):
    to_gx, to_x = routes()
    c = lax.axis_index("yz") % 2
    for i, j, k in CHIP_STEPS[1:]:
        action(to_gx[i][j], to_x[k], to_x[k] * 2 + c)


def meet_all():
    barrier = pltpu.get_barrier_semaphore()
    each_other_device(
        lambda to_gx, to_yz: pl.semaphore_signal(
            barrier, inc=1, device_id=(to_gx, to_yz), device_id_type=MESH
        )
    )
    pl.semaphore_wait(barrier, 127)


def send_to(src, dst, send_sem, recv_sem, to_gx, to_yz):
    pltpu.make_async_remote_copy(
        src_ref=src,
        dst_ref=dst,
        send_sem=send_sem,
        recv_sem=recv_sem,
        device_id=(to_gx, to_yz),
        device_id_type=MESH,
    ).start()


def wait_for(ref, sem):
    pltpu.make_async_copy(ref, ref, sem).wait()


def reciprocal(value):
    guess = pltpu.reciprocal(value, approx=True)
    return guess * (2.0 - value * guess)


def inverse_factor(cross):
    n = RANK
    row = lax.broadcasted_iota(jnp.int32, (n, n), 0)
    col = lax.broadcasted_iota(jnp.int32, (n, n), 1)
    eye = row == col
    diagonal = jnp.where(eye, cross, 0.0)
    scale_row = lax.rsqrt(jnp.sum(diagonal, axis=0, keepdims=True))
    scale_col = lax.rsqrt(jnp.sum(diagonal, axis=1, keepdims=True))
    a = cross * scale_row * scale_col
    e = jnp.where(eye, 1.0, 0.0)
    local = lax.broadcasted_iota(jnp.int32, (STRIP, n), 0)
    done = []
    for strip in range(n // STRIP):
        ra = a[STRIP * strip : STRIP * (strip + 1)]
        re = e[STRIP * strip : STRIP * (strip + 1)]
        alpha = jnp.zeros((STRIP, n), F32)
        beta = jnp.zeros((STRIP, n), F32)
        for panel in range(STRIP // PANEL):
            base = STRIP * strip + PANEL * panel
            c = [jnp.broadcast_to(ra[:, base + j : base + j + 1], (STRIP, n)) for j in range(PANEL)]
            for pair in range(PANEL // 2):
                k = PANEL * panel + 2 * pair
                c0, c1 = c[2 * pair], c[2 * pair + 1]
                p00, p01, p11 = c0[k : k + 1], c1[k : k + 1], c1[k + 1 : k + 2]
                det = p00 * p11 - p01 * p01
                inv = reciprocal(det)
                below = local > k + 1
                m0 = jnp.where(below, (c0 * p11 - c1 * p01) * inv, 0.0)
                m1 = jnp.where(below, (c1 * p00 - c0 * p01) * inv, 0.0)
                for j in range(2 * pair + 2, PANEL):
                    c[j] = c[j] - m0 * c[j][k : k + 1] - m1 * c[j][k + 1 : k + 2]
                if k + 2 < STRIP:
                    ra = ra - m0 * ra[k : k + 1] - m1 * ra[k + 1 : k + 2]
                    re = re - m0 * re[k : k + 1] - m1 * re[k + 1 : k + 2]
                s0 = lax.rsqrt(p00)
                s1 = lax.rsqrt(det * (s0 * s0))
                alpha = jnp.where(local == k, s0, jnp.where(local == k + 1, s1, alpha))
                beta = jnp.where(local == k + 1, p01 * (s0 * s0), beta)
        ua = alpha * (ra - beta * pltpu.roll(ra, 1, 0))
        ue = alpha * (re - beta * pltpu.roll(re, 1, 0))
        done.append(ue)
        if strip + 1 < n // STRIP:
            h, m, l = split3(jnp.concatenate([ua, ue], axis=1))
            left = jnp.concatenate([part[:, :n] for part in (h, h, m, h, m, l)], axis=0)
            right = jnp.concatenate([h, m, h, l, m, h], axis=0)
            update = dot(left, right, TN)
            a = a - update[:, :n]
            e = e - update[:, n:]
    return jnp.concatenate(done, axis=0) * scale_row


def kernel(
    field, start, basis, gram_y,
    landed, high, low, both, cross,
    half_gram, pair_gram, sum_gram, parts_gram, all_gram, gram_x,
    core, core_t, give, keep, pair_y,
    plane_y, line_y, line_sum, plane_sum, upper_y, lower_y,
    field_send, field_recv, gram_send, gram_recv, pair_send, pair_recv, y_send, y_recv,
):
    gx, yz, z, y, x, c = position()
    chip = gx * 4 + x
    meet_all()

    own = pl.ds(pl.multiple_of(yz * 512 + gx * 32, 32), 32)

    def exchange(r, carry):
        pltpu.make_async_copy(
            field.at[:, (gx * 8 + yz) * ROUNDS + r], landed.at[r, own], field_recv.at[r]
        ).start()
        each_other_device(
            lambda to_gx, to_yz: send_to(
                field.at[:, (to_gx * 8 + to_yz) * ROUNDS + r],
                landed.at[r, own],
                field_send.at[r],
                field_recv.at[r],
                to_gx,
                to_yz,
            )
        )
        return carry

    lax.fori_loop(0, ROUNDS, exchange, 0)

    for r in range(ROUNDS):
        wait_for(landed.at[r], field_recv.at[r])
        for j in range(8):
            h, l = split(landed[r, 512 * j : 512 * (j + 1), :])
            high[r, :, 128 * j : 128 * (j + 1)] = h
            low[r, :, 128 * j : 128 * (j + 1)] = l
        h, l = high[r], low[r]
        if r == 0:
            both[...] = dot(h, h, NT)
            cross[...] = dot(h, l, NT)
        else:
            both[...] += dot(h, h, NT)
            cross[...] += dot(h, l, NT)
    for j in range(4):
        columns = slice(128 * j, 128 * (j + 1))
        half_gram[512 * j : 512 * (j + 1), :] = 0.5 * both[:, columns] + cross[:, columns]

    mine = pl.ds(pl.multiple_of(c * 1024, 1024), 1024)
    other = pl.ds(pl.multiple_of((1 - c) * 1024, 1024), 1024)
    partner = x * 2 + 1 - c
    send_to(half_gram.at[other], pair_gram, gram_send.at[0], gram_recv.at[0], gx, partner)
    wait_for(pair_gram, gram_recv.at[0])
    sum_gram[...] = half_gram[mine, :] + pair_gram[...]
    each_other_chip(
        lambda to_gx, to_x, to_yz: send_to(
            sum_gram.at[pl.ds(pl.multiple_of((to_gx * 4 + to_x) * 16, 16), 16)],
            parts_gram.at[chip],
            gram_send.at[1],
            gram_recv.at[1],
            to_gx,
            to_yz,
        )
    )
    parts_gram[chip] = sum_gram[pl.ds(pl.multiple_of(chip * 16, 16), 16), :]
    wait_for(parts_gram.at[pl.ds(0, 63)], gram_recv.at[1])
    piece = pl.ds(pl.multiple_of(c * 1024 + chip * 16, 16), 16)
    all_gram[piece, :] = jnp.sum(parts_gram[...], axis=0)
    each_other_chip(
        lambda to_gx, to_x, to_yz: send_to(
            all_gram.at[piece], all_gram.at[piece], gram_send.at[2], gram_recv.at[2], to_gx, to_yz
        )
    )
    wait_for(all_gram.at[pl.ds(0, 63 * 16)], gram_recv.at[2])
    send_to(all_gram.at[mine], all_gram.at[mine], gram_send.at[3], gram_recv.at[3], gx, partner)
    wait_for(all_gram.at[other], gram_recv.at[3])
    total = jnp.concatenate([all_gram[512 * j : 512 * (j + 1), :] for j in range(4)], axis=1)
    gram_x[...] = (total + total.T) * (1.0 / (512 * 1024))

    def normaliser(product):
        return inverse_factor(dot_exact(product, product, NT))

    def iterate(step, product):
        ahead = dot_exact(product, gram_x[...], NN)
        return dot_exact(normaliser(product), ahead, NN)

    product = dot_exact(start[...].T, gram_x[...], NN)
    product = lax.fori_loop(0, ITERS - 1, iterate, product)
    rows = dot_exact(normaliser(product), product, NN)
    basis[...] = rows.T

    b_high, b_low = split(rows)
    for r in range(ROUNDS):
        h, l = high[r], low[r]
        part = dot(b_high, h, NN) + (dot(b_high, l, NN) + dot(b_low, h, NN))
        h, l = split(part)
        for n, piece in enumerate((h, l, h)):
            core[512 * n + RANK * r : 512 * n + RANK * (r + 1), :] = piece
        h, l = split(part.T)
        for n, piece in enumerate((h, h, l)):
            core_t[:, 512 * n + RANK * r : 512 * n + RANK * (r + 1)] = piece

    def columns_of(parity, block, n):
        pair = [core[:, pl.ds(pl.multiple_of((2 * j + parity) * 128, 128), 128)] for j in (2 * n, 2 * n + 1)]
        value = dot(core_t[...], jnp.concatenate(pair, axis=1), NN)
        block[2 * n] = value[:, :128].reshape(16, 64, 128)
        block[2 * n + 1] = value[:, 128:].reshape(16, 64, 128)

    for n in range(2):
        columns_of(1 - c, give, n)
        pair_half = pair_y.at[pl.ds(2 * n, 2)]
        send_to(give.at[pl.ds(2 * n, 2)], pair_half, pair_send.at[n], pair_recv.at[n], gx, partner)
    for n in range(2):
        columns_of(c, keep, n)
    for n in range(2):
        wait_for(pair_y.at[pl.ds(2 * n, 2)], pair_recv.at[n])
        keep[2 * n : 2 * n + 2] = keep[2 * n : 2 * n + 2] + pair_y[2 * n : 2 * n + 2]

    to_gx, to_x = routes()
    plane = [to_gx[i][(a + i) % 4] for a in range(4) for i in range(4)][1:]

    first, second = pl.ds(0, 32), pl.ds(32, 32)
    for n, at in enumerate(plane):
        send_to(keep.at[:, at, second], plane_y.at[gx], y_send.at[0], y_recv.at[0], at, yz)
        if n % 5 == 0:
            to = to_x[1 + n // 5]
            send_to(keep.at[to, :, first], line_y.at[x], y_send.at[1], y_recv.at[1], gx, 2 * to + c)
    plane_y[gx] = keep[:, gx, 32:, :]
    line_y[x] = keep[x, :, :32, :]
    wait_for(line_y.at[pl.ds(0, 3)], y_recv.at[1])
    line_sum[...] = jnp.sum(line_y[...], axis=0)
    for at in plane:
        send_to(line_sum.at[at], upper_y.at[gx], y_send.at[2], y_recv.at[2], at, yz)
    wait_for(plane_y.at[pl.ds(0, 15)], y_recv.at[0])
    plane_sum[...] = jnp.sum(plane_y[...], axis=0)
    for at in to_x[1:]:
        send_to(plane_sum.at[at], lower_y.at[x], y_send.at[3], y_recv.at[3], gx, 2 * at + c)
    upper_y[gx] = line_sum[gx]
    lower_y[x] = plane_sum[x]
    wait_for(upper_y.at[pl.ds(0, 15)], y_recv.at[2])
    wait_for(lower_y.at[pl.ds(0, 3)], y_recv.at[3])
    gram_y[0:32, :] = jnp.sum(upper_y[...], axis=0) * (1.0 / 65536)
    gram_y[32:64, :] = jnp.sum(lower_y[...], axis=0) * (1.0 / 65536)

    for r in range(ROUNDS):
        wait_for(landed.at[r, pl.ds(0, 127 * 32)], field_send.at[r])
    wait_for(pair_gram, gram_send.at[0])
    wait_for(parts_gram.at[pl.ds(0, 63)], gram_send.at[1])
    wait_for(parts_gram.at[pl.ds(0, 63)], gram_send.at[2])
    wait_for(all_gram.at[mine], gram_send.at[3])
    for n in range(2):
        wait_for(give.at[pl.ds(2 * n, 2)], pair_send.at[n])
    wait_for(plane_y.at[pl.ds(0, 15)], y_send.at[0])
    wait_for(line_y.at[pl.ds(0, 3)], y_send.at[1])
    wait_for(upper_y.at[pl.ds(0, 15)], y_send.at[2])
    wait_for(lower_y.at[pl.ds(0, 3)], y_send.at[3])


def on_device(field, start):
    vmem = pl.BlockSpec(memory_space=pltpu.VMEM)
    basis, piece = pl.pallas_call(
        kernel,
        out_shape=(
            jax.ShapeDtypeStruct((512, RANK), F32),
            jax.ShapeDtypeStruct((64, 128), F32),
        ),
        in_specs=[pl.BlockSpec(memory_space=pl.ANY), vmem],
        out_specs=(vmem, vmem),
        scratch_shapes=[
            pltpu.VMEM((ROUNDS, 4096, 128), F32),
            pltpu.VMEM((ROUNDS, 512, 1024), BF16),
            pltpu.VMEM((ROUNDS, 512, 1024), BF16),
            pltpu.VMEM((512, 512), F32),
            pltpu.VMEM((512, 512), F32),
            pltpu.VMEM((2048, 128), F32),
            pltpu.VMEM((1024, 128), F32),
            pltpu.VMEM((1024, 128), F32),
            pltpu.VMEM((64, 16, 128), F32),
            pltpu.VMEM((2048, 128), F32),
            pltpu.VMEM((512, 512), F32),
            pltpu.VMEM((1536, 1024), BF16),
            pltpu.VMEM((1024, 1536), BF16),
            pltpu.VMEM((4, 16, 64, 128), F32),
            pltpu.VMEM((4, 16, 64, 128), F32),
            pltpu.VMEM((4, 16, 64, 128), F32),
            pltpu.VMEM((16, 4, 32, 128), F32),
            pltpu.VMEM((4, 16, 32, 128), F32),
            pltpu.VMEM((16, 32, 128), F32),
            pltpu.VMEM((4, 32, 128), F32),
            pltpu.VMEM((16, 32, 128), F32),
            pltpu.VMEM((4, 32, 128), F32),
            pltpu.SemaphoreType.DMA((ROUNDS,)),
            pltpu.SemaphoreType.DMA((ROUNDS,)),
            pltpu.SemaphoreType.DMA((4,)),
            pltpu.SemaphoreType.DMA((4,)),
            pltpu.SemaphoreType.DMA((2,)),
            pltpu.SemaphoreType.DMA((2,)),
            pltpu.SemaphoreType.DMA((4,)),
            pltpu.SemaphoreType.DMA((4,)),
        ],
        compiler_params=pltpu.CompilerParams(
            collective_id=0, has_side_effects=True, vmem_limit_bytes=56 << 20
        ),
    )(field, start)
    return basis, piece.T


def solution(mesh):
    placed = (P("gx", None, "yz"), P())
    return jax.shard_map(
        on_device, mesh=mesh, in_specs=placed, out_specs=(P(), P("yz", "gx")), check_vma=False
    )
```

```python
import functools

import jax
import jax.numpy as jnp
from jax import lax
from jax.experimental import pallas as pl
from jax.experimental.pallas import tpu as pltpu
from jax.sharding import PartitionSpec as P

ITERS = 4
ROUNDS = 4
RANK = 128
STRIP = 32
PANEL = 16
F32 = jnp.float32
BF16 = jnp.bfloat16
MESH = pl.DeviceIdType.MESH
NN = (((1,), (0,)), ((), ()))
NT = (((1,), (1,)), ((), ()))
TN = (((0,), (0,)), ((), ()))
BLOCKS = [(0, 0), (1, 0), (2, 0), (3, 0), (1, 1), (2, 1), (3, 1), (2, 2), (3, 2), (3, 3)]


def dot(left, right, dims, precision=None):
    return lax.dot_general(left, right, dims, precision=precision, preferred_element_type=F32)


def dot_exact(left, right, dims):
    return dot(left, right, dims, lax.Precision.HIGHEST)


def split(value):
    high = value.astype(BF16)
    return high, (value - high.astype(F32)).astype(BF16)


def split3(value):
    high = value.astype(BF16)
    rest = value - high.astype(F32)
    return (high,) + split(rest)


def position():
    gx, yz = lax.axis_index("gx"), lax.axis_index("yz")
    return gx, yz, gx // 4, gx % 4, yz // 2, yz % 2


def routes():
    gx, yz, z, y, x, c = position()
    sign = 1 + 2 * c
    to_z, to_y, to_x = ([(at + sign * i) % 4 for i in range(4)] for at in (z, y, x))
    return [[to_z[i] * 4 + to_y[j] for j in range(4)] for i in range(4)], to_x


CHIP_STEPS = [(i, (a + i) % 4, (b + i) % 4) for b in range(4) for a in range(4) for i in range(4)]


def each_other_device(action):
    to_gx, to_x = routes()
    c = lax.axis_index("yz") % 2
    to_x = [jnp.where(c == 0, to_x[i], to_x[(i + 2) % 4]) for i in range(4)]
    to_yz = [[2 * at + c for at in to_x], [2 * at + 1 - c for at in to_x]]
    for group in range(16):
        for flip in range(2):
            for i, j, k in CHIP_STEPS[4 * group : 4 * group + 4]:
                act = functools.partial(action, to_gx[i][j], to_yz[flip][k])
                if (i, j, k % 2, flip) == (0, 0, 0, 0):
                    pl.when(c != k // 2)(act)
                else:
                    act()


def each_other_chip(action):
    to_gx, to_x = routes()
    c = lax.axis_index("yz") % 2
    for i, j, k in CHIP_STEPS[1:]:
        action((i, j, k), to_gx[i][j], to_x[k], to_x[k] * 2 + c)


def meet_all():
    barrier = pltpu.get_barrier_semaphore()
    each_other_device(
        lambda to_gx, to_yz: pl.semaphore_signal(
            barrier, inc=1, device_id=(to_gx, to_yz), device_id_type=MESH
        )
    )
    pl.semaphore_wait(barrier, 127)


def send_to(src, dst, send_sem, recv_sem, to_gx, to_yz):
    pltpu.make_async_remote_copy(
        src_ref=src,
        dst_ref=dst,
        send_sem=send_sem,
        recv_sem=recv_sem,
        device_id=(to_gx, to_yz),
        device_id_type=MESH,
    ).start()


def wait_for(ref, sem):
    pltpu.make_async_copy(ref, ref, sem).wait()


def inverse_factor(cross):
    n = RANK
    row = lax.broadcasted_iota(jnp.int32, (n, n), 0)
    col = lax.broadcasted_iota(jnp.int32, (n, n), 1)
    eye = row == col
    diagonal = jnp.where(eye, cross, 0.0)
    scale_row = lax.rsqrt(jnp.sum(diagonal, axis=0, keepdims=True))
    scale_col = lax.rsqrt(jnp.sum(diagonal, axis=1, keepdims=True))
    a = cross * scale_row * scale_col
    e = jnp.where(eye, 1.0, 0.0)
    local = lax.broadcasted_iota(jnp.int32, (STRIP, n), 0)
    done = []
    for strip in range(n // STRIP):
        ra = a[STRIP * strip : STRIP * (strip + 1)]
        re = e[STRIP * strip : STRIP * (strip + 1)]
        alpha = jnp.zeros((STRIP, n), F32)
        beta = jnp.zeros((STRIP, n), F32)
        for panel in range(STRIP // PANEL):
            base = STRIP * strip + PANEL * panel
            c = [jnp.broadcast_to(ra[:, base + j : base + j + 1], (STRIP, n)) for j in range(PANEL)]
            for pair in range(PANEL // 2):
                k = PANEL * panel + 2 * pair
                c0, c1 = c[2 * pair], c[2 * pair + 1]
                p00, p01, p11 = c0[k : k + 1], c1[k : k + 1], c1[k + 1 : k + 2]
                det = p00 * p11 - p01 * p01
                inv = pltpu.reciprocal(det, approx=True)
                below = local > k + 1
                n0 = jnp.where(below, c0 * p11 - c1 * p01, 0.0)
                n1 = jnp.where(below, c1 * p00 - c0 * p01, 0.0)
                m0, m1 = n0 * inv, n1 * inv
                for j in range(2 * pair + 2, min(2 * pair + 4, PANEL)):
                    c[j] = c[j] - (n0 * c[j][k : k + 1] + n1 * c[j][k + 1 : k + 2]) * inv
                for j in range(2 * pair + 4, PANEL):
                    c[j] = c[j] - m0 * c[j][k : k + 1] - m1 * c[j][k + 1 : k + 2]
                if k + 2 < STRIP:
                    ra = ra - m0 * ra[k : k + 1] - m1 * ra[k + 1 : k + 2]
                    re = re - m0 * re[k : k + 1] - m1 * re[k + 1 : k + 2]
                s0 = lax.rsqrt(p00)
                s1 = lax.rsqrt(det * (s0 * s0))
                alpha = jnp.where(local == k, s0, jnp.where(local == k + 1, s1, alpha))
                beta = jnp.where(local == k + 1, p01 * (s0 * s0), beta)
        ua = alpha * (ra - beta * pltpu.roll(ra, 1, 0))
        ue = alpha * (re - beta * pltpu.roll(re, 1, 0))
        done.append(ue)
        if strip + 1 < n // STRIP:
            h, m, l = split3(jnp.concatenate([ua, ue], axis=1))
            left = jnp.concatenate([part[:, :n] for part in (h, h, m, h, m, l)], axis=0)
            right = jnp.concatenate([h, m, h, l, m, h], axis=0)
            update = dot(left, right, TN)
            a = a - update[:, :n]
            e = e - update[:, n:]
    return jnp.concatenate(done, axis=0) * scale_row


def kernel(
    field, start, basis, gram_y,
    landed, high, low, left_half, right_half,
    own_gram, pair_gram, sum_gram, parts_gram, all_gram, gram_x,
    core, core_t, give, keep, pair_y,
    plane_y, line_y, line_sum, plane_sum, upper_y, lower_y,
    field_send, field_recv, gram_send, gram_recv, pair_send, pair_recv, y_send, y_recv,
):
    gx, yz, z, y, x, c = position()
    chip = gx * 4 + x
    meet_all()

    own = pl.ds(pl.multiple_of(yz * 512 + gx * 32, 32), 32)

    def exchange(r, carry):
        pltpu.make_async_copy(
            field.at[:, (gx * 8 + yz) * ROUNDS + r], landed.at[r, own], field_recv.at[r]
        ).start()
        each_other_device(
            lambda to_gx, to_yz: send_to(
                field.at[:, (to_gx * 8 + to_yz) * ROUNDS + r],
                landed.at[r, own],
                field_send.at[r],
                field_recv.at[r],
                to_gx,
                to_yz,
            )
        )
        return carry

    lax.fori_loop(0, ROUNDS, exchange, 0)

    for r in range(ROUNDS):
        wait_for(landed.at[r], field_recv.at[r])
        for j in range(8):
            h, l = split(landed[r, 512 * j : 512 * (j + 1), :])
            high[r, :, 128 * j : 128 * (j + 1)] = h
            low[r, :, 128 * j : 128 * (j + 1)] = l
        h, l = high[r], low[r]
        left = jnp.concatenate([h, h, l], axis=1)
        right = jnp.concatenate([h, l, h], axis=1)
        if r == 0:
            left_half[...] = dot(left, right[:256], NT)
            right_half[...] = dot(left[256:], right[256:], NT)
        else:
            left_half[...] += dot(left, right[:256], NT)
            right_half[...] += dot(left[256:], right[256:], NT)
    for n, (i, j) in enumerate(BLOCKS):
        if j < 2:
            block = left_half[128 * i : 128 * (i + 1), 128 * j : 128 * (j + 1)]
        else:
            block = right_half[128 * (i - 2) : 128 * (i - 1), 128 * (j - 2) : 128 * (j - 1)]
        own_gram[128 * n : 128 * (n + 1), :] = block

    def half(of):
        return pl.ds(pl.multiple_of(of * 640, 128), 640)

    def rows_of(at, place, size):
        start = at * 40 + jnp.where(place == 0, 0, 8 + 8 * place)
        return pl.ds(pl.multiple_of(start, 8), size)

    place = (x + 8 - z - y) % 4
    wide = place == 0
    partner = x * 2 + 1 - c
    send_to(own_gram.at[half(1 - c)], pair_gram, gram_send.at[0], gram_recv.at[0], gx, partner)
    wait_for(pair_gram, gram_recv.at[0])
    sum_gram[...] = own_gram[half(c), :] + pair_gram[...]
    places = [(place + (1 + 2 * c) * n) % 4 for n in range(4)]

    def scatter(steps, to_gx, to_x, to_yz):
        to_place = places[(steps[2] - steps[0] - steps[1]) % 4]

        def part(size):
            send_to(
                sum_gram.at[rows_of(to_gx, to_place, size)], parts_gram.at[chip, pl.ds(0, size)],
                gram_send.at[1], gram_recv.at[1], to_gx, to_yz,
            )

        pl.when(to_place == 0)(lambda: part(16))
        pl.when(to_place != 0)(lambda: part(8))

    each_other_chip(scatter)

    def finish(size):
        mine = rows_of(gx, place, size)
        parts_gram[chip, 0:size] = sum_gram[mine, :]
        wait_for(parts_gram.at[pl.ds(0, 63), pl.ds(0, size)], gram_recv.at[1])
        piece = pl.ds(pl.multiple_of(c * 640 + mine.start, 8), size)
        all_gram[piece, :] = jnp.sum(parts_gram[:, 0:size], axis=0)
        each_other_chip(
            lambda steps, to_gx, to_x, to_yz: send_to(
                all_gram.at[piece], all_gram.at[piece], gram_send.at[2], gram_recv.at[2], to_gx, to_yz
            )
        )
        wait_for(all_gram.at[pl.ds(0, 640 - size)], gram_recv.at[2])

    pl.when(wide)(lambda: finish(16))
    pl.when(jnp.logical_not(wide))(lambda: finish(8))
    send_to(all_gram.at[half(c)], all_gram.at[half(c)], gram_send.at[3], gram_recv.at[3], gx, partner)
    wait_for(all_gram.at[half(1 - c)], gram_recv.at[3])
    for n, (i, j) in enumerate(BLOCKS):
        block = all_gram[128 * n : 128 * (n + 1), :] * (1.0 / (512 * 1024))
        gram_x[128 * i : 128 * (i + 1), 128 * j : 128 * (j + 1)] = block
        if i != j:
            gram_x[128 * j : 128 * (j + 1), 128 * i : 128 * (i + 1)] = block.T

    def normaliser(product):
        return inverse_factor(dot_exact(product, product, NT))

    def iterate(step, product):
        ahead = dot_exact(product, gram_x[...], NN)
        return dot_exact(normaliser(product), ahead, NN)

    product = dot_exact(start[...].T, gram_x[...], NN)
    product = lax.fori_loop(0, ITERS - 1, iterate, product)
    rows = dot_exact(normaliser(product), product, NN)
    basis[...] = rows.T

    b_high, b_low = split(rows)
    for r in range(ROUNDS):
        h, l = high[r], low[r]
        part = dot(b_high, h, NN) + (dot(b_high, l, NN) + dot(b_low, h, NN))
        h, l = split(part)
        for n, piece in enumerate((h, l, h)):
            core[512 * n + RANK * r : 512 * n + RANK * (r + 1), :] = piece
        h, l = split(part.T)
        for n, piece in enumerate((h, h, l)):
            core_t[:, 512 * n + RANK * r : 512 * n + RANK * (r + 1)] = piece

    def columns_of(parity, block, n):
        pair = [core[:, pl.ds(pl.multiple_of((2 * j + parity) * 128, 128), 128)] for j in (2 * n, 2 * n + 1)]
        value = dot(core_t[...], jnp.concatenate(pair, axis=1), NN)
        block[2 * n] = value[:, :128].reshape(16, 64, 128)
        block[2 * n + 1] = value[:, 128:].reshape(16, 64, 128)

    for n in range(2):
        columns_of(1 - c, give, n)
        pair_half = pair_y.at[pl.ds(2 * n, 2)]
        send_to(give.at[pl.ds(2 * n, 2)], pair_half, pair_send.at[n], pair_recv.at[n], gx, partner)
    for n in range(2):
        columns_of(c, keep, n)
    for n in range(2):
        wait_for(pair_y.at[pl.ds(2 * n, 2)], pair_recv.at[n])
        keep[2 * n : 2 * n + 2] = keep[2 * n : 2 * n + 2] + pair_y[2 * n : 2 * n + 2]

    to_gx, to_x = routes()
    plane = [to_gx[i][(a + i) % 4] for a in range(4) for i in range(4)][1:]

    first, second = pl.ds(0, 32), pl.ds(32, 32)
    for n, at in enumerate(plane):
        send_to(keep.at[:, at, second], plane_y.at[gx], y_send.at[0], y_recv.at[0], at, yz)
        if n % 5 == 0:
            to = to_x[1 + n // 5]
            send_to(keep.at[to, :, first], line_y.at[x], y_send.at[1], y_recv.at[1], gx, 2 * to + c)
    plane_y[gx] = keep[:, gx, 32:, :]
    line_y[x] = keep[x, :, :32, :]
    wait_for(line_y.at[pl.ds(0, 3)], y_recv.at[1])
    line_sum[...] = jnp.sum(line_y[...], axis=0)
    for at in plane:
        send_to(line_sum.at[at], upper_y.at[gx], y_send.at[2], y_recv.at[2], at, yz)
    wait_for(plane_y.at[pl.ds(0, 15)], y_recv.at[0])
    plane_sum[...] = jnp.sum(plane_y[...], axis=0)
    for at in to_x[1:]:
        send_to(plane_sum.at[at], lower_y.at[x], y_send.at[3], y_recv.at[3], gx, 2 * at + c)
    upper_y[gx] = line_sum[gx]
    lower_y[x] = plane_sum[x]
    wait_for(upper_y.at[pl.ds(0, 15)], y_recv.at[2])
    wait_for(lower_y.at[pl.ds(0, 3)], y_recv.at[3])
    gram_y[0:32, :] = jnp.sum(upper_y[...], axis=0) * (1.0 / 65536)
    gram_y[32:64, :] = jnp.sum(lower_y[...], axis=0) * (1.0 / 65536)

    for r in range(ROUNDS):
        wait_for(landed.at[r, pl.ds(0, 127 * 32)], field_send.at[r])
    wait_for(pair_gram, gram_send.at[0])
    pl.when(wide)(lambda: wait_for(own_gram.at[pl.ds(0, 15 * 16 + 48 * 8)], gram_send.at[1]))
    pl.when(jnp.logical_not(wide))(lambda: wait_for(own_gram.at[pl.ds(0, 16 * 16 + 47 * 8)], gram_send.at[1]))
    pl.when(wide)(lambda: wait_for(parts_gram.at[pl.ds(0, 63)], gram_send.at[2]))
    pl.when(jnp.logical_not(wide))(lambda: wait_for(parts_gram.at[pl.ds(0, 63), pl.ds(0, 8)], gram_send.at[2]))
    wait_for(all_gram.at[half(c)], gram_send.at[3])
    for n in range(2):
        wait_for(give.at[pl.ds(2 * n, 2)], pair_send.at[n])
    wait_for(plane_y.at[pl.ds(0, 15)], y_send.at[0])
    wait_for(line_y.at[pl.ds(0, 3)], y_send.at[1])
    wait_for(upper_y.at[pl.ds(0, 15)], y_send.at[2])
    wait_for(lower_y.at[pl.ds(0, 3)], y_send.at[3])


def deliver(basis, piece, basis_out, piece_out):
    basis_out[...] = basis[...]
    piece_out[...] = piece[...]


def on_device(field, start):
    vmem = pl.BlockSpec(memory_space=pltpu.VMEM)
    basis, piece = pl.pallas_call(
        kernel,
        out_shape=(
            jax.ShapeDtypeStruct((512, RANK), F32),
            jax.ShapeDtypeStruct((64, 128), F32),
        ),
        in_specs=[pl.BlockSpec(memory_space=pl.ANY), vmem],
        out_specs=(vmem, vmem),
        scratch_shapes=[
            pltpu.VMEM((ROUNDS, 4096, 128), F32),
            pltpu.VMEM((ROUNDS, 512, 1024), BF16),
            pltpu.VMEM((ROUNDS, 512, 1024), BF16),
            pltpu.VMEM((512, 256), F32),
            pltpu.VMEM((256, 256), F32),
            pltpu.VMEM((1280, 128), F32),
            pltpu.VMEM((640, 128), F32),
            pltpu.VMEM((640, 128), F32),
            pltpu.VMEM((64, 16, 128), F32),
            pltpu.VMEM((1280, 128), F32),
            pltpu.VMEM((512, 512), F32),
            pltpu.VMEM((1536, 1024), BF16),
            pltpu.VMEM((1024, 1536), BF16),
            pltpu.VMEM((4, 16, 64, 128), F32),
            pltpu.VMEM((4, 16, 64, 128), F32),
            pltpu.VMEM((4, 16, 64, 128), F32),
            pltpu.VMEM((16, 4, 32, 128), F32),
            pltpu.VMEM((4, 16, 32, 128), F32),
            pltpu.VMEM((16, 32, 128), F32),
            pltpu.VMEM((4, 32, 128), F32),
            pltpu.VMEM((16, 32, 128), F32),
            pltpu.VMEM((4, 32, 128), F32),
            pltpu.SemaphoreType.DMA((ROUNDS,)),
            pltpu.SemaphoreType.DMA((ROUNDS,)),
            pltpu.SemaphoreType.DMA((4,)),
            pltpu.SemaphoreType.DMA((4,)),
            pltpu.SemaphoreType.DMA((2,)),
            pltpu.SemaphoreType.DMA((2,)),
            pltpu.SemaphoreType.DMA((4,)),
            pltpu.SemaphoreType.DMA((4,)),
        ],
        compiler_params=pltpu.CompilerParams(
            collective_id=0, has_side_effects=True, vmem_limit_bytes=56 << 20
        ),
    )(field, start)
    basis, piece = pl.pallas_call(
        deliver,
        out_shape=(
            jax.ShapeDtypeStruct((512, RANK), F32),
            jax.ShapeDtypeStruct((64, 128), F32),
        ),
        in_specs=[vmem, vmem],
        out_specs=(vmem, vmem),
    )(basis, piece)
    return basis, piece.T


def solution(mesh):
    placed = (P("gx", None, "yz"), P())
    return jax.shard_map(
        on_device, mesh=mesh, in_specs=placed, out_specs=(P(), P("yz", "gx")), check_vma=False
    )
```

```python
import functools

import jax
import jax.numpy as jnp
from jax import lax
from jax.experimental import pallas as pl
from jax.experimental.pallas import tpu as pltpu
from jax.sharding import PartitionSpec as P

ITERS = 4
ROUNDS = 4
RANK = 128
STRIP = 32
PANEL = 16
F32 = jnp.float32
BF16 = jnp.bfloat16
MESH = pl.DeviceIdType.MESH
NN = (((1,), (0,)), ((), ()))
NT = (((1,), (1,)), ((), ()))
TN = (((0,), (0,)), ((), ()))
BLOCKS = [(0, 0), (1, 0), (2, 0), (3, 0), (1, 1), (2, 1), (3, 1), (2, 2), (3, 2), (3, 3)]


def dot(left, right, dims, precision=None):
    return lax.dot_general(left, right, dims, precision=precision, preferred_element_type=F32)


def dot_exact(left, right, dims):
    return dot(left, right, dims, lax.Precision.HIGHEST)


def split(value):
    high = value.astype(BF16)
    return high, (value - high.astype(F32)).astype(BF16)


def split3(value):
    high = value.astype(BF16)
    rest = value - high.astype(F32)
    return (high,) + split(rest)


def stacked(value, order, axis):
    parts = split3(value)
    return jnp.concatenate([parts[n] for n in order], axis=axis)


def dot_six(left, right):
    return dot(stacked(left, (0, 0, 1, 0, 1, 2), 1), stacked(right, (0, 1, 0, 2, 1, 0), 0), NN)


def row_gram(value):
    high, middle, low = split3(value)
    mixed = dot(high, middle, NT) + dot(high, low, NT)
    both = jnp.concatenate([high, middle], axis=1)
    return dot(both, both, NT) + (mixed + mixed.T)


def position():
    gx, yz = lax.axis_index("gx"), lax.axis_index("yz")
    return gx, yz, gx // 4, gx % 4, yz // 2, yz % 2


def routes():
    gx, yz, z, y, x, c = position()
    sign = 1 + 2 * c
    to_z, to_y, to_x = ([(at + sign * i) % 4 for i in range(4)] for at in (z, y, x))
    return [[to_z[i] * 4 + to_y[j] for j in range(4)] for i in range(4)], to_x


CHIP_STEPS = [(i, (a + i) % 4, (b + i) % 4) for b in range(4) for a in range(4) for i in range(4)]


def each_other_device(action):
    to_gx, to_x = routes()
    c = lax.axis_index("yz") % 2
    to_x = [jnp.where(c == 0, to_x[i], to_x[(i + 2) % 4]) for i in range(4)]
    to_yz = [[2 * at + c for at in to_x], [2 * at + 1 - c for at in to_x]]
    for group in range(16):
        for flip in range(2):
            for i, j, k in CHIP_STEPS[4 * group : 4 * group + 4]:
                act = functools.partial(action, to_gx[i][j], to_yz[flip][k])
                if (i, j, k % 2, flip) == (0, 0, 0, 0):
                    pl.when(c != k // 2)(act)
                else:
                    act()


def each_other_chip(action):
    to_gx, to_x = routes()
    c = lax.axis_index("yz") % 2
    for i, j, k in CHIP_STEPS[1:]:
        action((i, j, k), to_gx[i][j], to_x[k], to_x[k] * 2 + c)


def meet_all():
    barrier = pltpu.get_barrier_semaphore()
    each_other_device(
        lambda to_gx, to_yz: pl.semaphore_signal(
            barrier, inc=1, device_id=(to_gx, to_yz), device_id_type=MESH
        )
    )
    pl.semaphore_wait(barrier, 127)


def send_to(src, dst, send_sem, recv_sem, to_gx, to_yz):
    pltpu.make_async_remote_copy(
        src_ref=src,
        dst_ref=dst,
        send_sem=send_sem,
        recv_sem=recv_sem,
        device_id=(to_gx, to_yz),
        device_id_type=MESH,
    ).start()


def wait_for(ref, sem):
    pltpu.make_async_copy(ref, ref, sem).wait()


def inverse_factor(cross):
    n = RANK
    row = lax.broadcasted_iota(jnp.int32, (n, n), 0)
    col = lax.broadcasted_iota(jnp.int32, (n, n), 1)
    eye = row == col
    diagonal = jnp.where(eye, cross, 0.0)
    scale_row = lax.rsqrt(jnp.sum(diagonal, axis=0, keepdims=True))
    scale_col = lax.rsqrt(jnp.sum(diagonal, axis=1, keepdims=True))
    a = cross * scale_row * scale_col
    e = jnp.where(eye, 1.0, 0.0)
    local = lax.broadcasted_iota(jnp.int32, (STRIP, n), 0)
    done = []
    for strip in range(n // STRIP):
        ra = a[STRIP * strip : STRIP * (strip + 1)]
        re = e[STRIP * strip : STRIP * (strip + 1)]
        alpha = jnp.zeros((STRIP, n), F32)
        beta = jnp.zeros((STRIP, n), F32)
        for panel in range(STRIP // PANEL):
            base = STRIP * strip + PANEL * panel
            c = [jnp.broadcast_to(ra[:, base + j : base + j + 1], (STRIP, n)) for j in range(PANEL)]
            for pair in range(PANEL // 2):
                k = PANEL * panel + 2 * pair
                c0, c1 = c[2 * pair], c[2 * pair + 1]
                p00, p01, p11 = c0[k : k + 1], c1[k : k + 1], c1[k + 1 : k + 2]
                det = p00 * p11 - p01 * p01
                inv = pltpu.reciprocal(det, approx=True)
                below = local > k + 1
                n0 = jnp.where(below, c0 * p11 - c1 * p01, 0.0)
                n1 = jnp.where(below, c1 * p00 - c0 * p01, 0.0)
                m0, m1 = n0 * inv, n1 * inv
                for j in range(2 * pair + 2, min(2 * pair + 4, PANEL)):
                    c[j] = c[j] - (n0 * c[j][k : k + 1] + n1 * c[j][k + 1 : k + 2]) * inv
                for j in range(2 * pair + 4, PANEL):
                    c[j] = c[j] - m0 * c[j][k : k + 1] - m1 * c[j][k + 1 : k + 2]
                if k + 2 < STRIP:
                    ra = ra - m0 * ra[k : k + 1] - m1 * ra[k + 1 : k + 2]
                    re = re - m0 * re[k : k + 1] - m1 * re[k + 1 : k + 2]
                s0 = lax.rsqrt(p00)
                s1 = lax.rsqrt(det * (s0 * s0))
                alpha = jnp.where(local == k, s0, jnp.where(local == k + 1, s1, alpha))
                beta = jnp.where(local == k + 1, p01 * (s0 * s0), beta)
        ua = alpha * (ra - beta * pltpu.roll(ra, 1, 0))
        ue = alpha * (re - beta * pltpu.roll(re, 1, 0))
        done.append(ue)
        if strip + 1 < n // STRIP:
            left = stacked(ua, (0, 0, 1, 0, 1, 2), 0)
            right = stacked(jnp.concatenate([ua, ue], axis=1), (0, 1, 0, 2, 1, 0), 0)
            update = dot(left, right, TN)
            a = a - update[:, :n]
            e = e - update[:, n:]
    return jnp.concatenate(done, axis=0) * scale_row


def kernel(
    field, start, basis, gram_y,
    landed, high, low, left_half, right_half,
    own_gram, pair_gram, sum_gram, parts_gram, all_gram, gram_x,
    core, core_t, give, keep, pair_y,
    plane_y, line_y, line_sum, plane_sum, upper_y, lower_y,
    field_send, field_recv, gram_send, gram_recv, pair_send, pair_recv, y_send, y_recv,
):
    gx, yz, z, y, x, c = position()
    chip = gx * 4 + x
    meet_all()

    own = pl.ds(pl.multiple_of(yz * 512 + gx * 32, 32), 32)

    def exchange(r, carry):
        pltpu.make_async_copy(
            field.at[:, (gx * 8 + yz) * ROUNDS + r], landed.at[r, own], field_recv.at[r]
        ).start()
        each_other_device(
            lambda to_gx, to_yz: send_to(
                field.at[:, (to_gx * 8 + to_yz) * ROUNDS + r],
                landed.at[r, own],
                field_send.at[r],
                field_recv.at[r],
                to_gx,
                to_yz,
            )
        )
        return carry

    lax.fori_loop(0, ROUNDS, exchange, 0)

    for r in range(ROUNDS):
        wait_for(landed.at[r], field_recv.at[r])
        for j in range(8):
            h, l = split(landed[r, 512 * j : 512 * (j + 1), :])
            high[r, :, 128 * j : 128 * (j + 1)] = h
            low[r, :, 128 * j : 128 * (j + 1)] = l
        h, l = high[r], low[r]
        left = jnp.concatenate([h, h, l], axis=1)
        right = jnp.concatenate([h, l, h], axis=1)
        if r == 0:
            left_half[...] = dot(left, right[:256], NT)
            right_half[...] = dot(left[256:], right[256:], NT)
        else:
            left_half[...] += dot(left, right[:256], NT)
            right_half[...] += dot(left[256:], right[256:], NT)
    for n, (i, j) in enumerate(BLOCKS):
        if j < 2:
            block = left_half[128 * i : 128 * (i + 1), 128 * j : 128 * (j + 1)]
        else:
            block = right_half[128 * (i - 2) : 128 * (i - 1), 128 * (j - 2) : 128 * (j - 1)]
        own_gram[128 * n : 128 * (n + 1), :] = block

    def half(of):
        return pl.ds(pl.multiple_of(of * 640, 128), 640)

    def rows_of(at, place, size):
        start = at * 40 + jnp.where(place == 0, 0, 8 + 8 * place)
        return pl.ds(pl.multiple_of(start, 8), size)

    place = (x + 8 - z - y) % 4
    wide = place == 0
    partner = x * 2 + 1 - c
    send_to(own_gram.at[half(1 - c)], pair_gram, gram_send.at[0], gram_recv.at[0], gx, partner)
    wait_for(pair_gram, gram_recv.at[0])
    sum_gram[...] = own_gram[half(c), :] + pair_gram[...]
    places = [(place + (1 + 2 * c) * n) % 4 for n in range(4)]

    def scatter(steps, to_gx, to_x, to_yz):
        to_place = places[(steps[2] - steps[0] - steps[1]) % 4]

        def part(size):
            send_to(
                sum_gram.at[rows_of(to_gx, to_place, size)], parts_gram.at[chip, pl.ds(0, size)],
                gram_send.at[1], gram_recv.at[1], to_gx, to_yz,
            )

        pl.when(to_place == 0)(lambda: part(16))
        pl.when(to_place != 0)(lambda: part(8))

    each_other_chip(scatter)

    def finish(size):
        mine = rows_of(gx, place, size)
        parts_gram[chip, 0:size] = sum_gram[mine, :]
        wait_for(parts_gram.at[pl.ds(0, 63), pl.ds(0, size)], gram_recv.at[1])
        piece = pl.ds(pl.multiple_of(c * 640 + mine.start, 8), size)
        all_gram[piece, :] = jnp.sum(parts_gram[:, 0:size], axis=0)
        each_other_chip(
            lambda steps, to_gx, to_x, to_yz: send_to(
                all_gram.at[piece], all_gram.at[piece], gram_send.at[2], gram_recv.at[2], to_gx, to_yz
            )
        )
        wait_for(all_gram.at[pl.ds(0, 640 - size)], gram_recv.at[2])

    pl.when(wide)(lambda: finish(16))
    pl.when(jnp.logical_not(wide))(lambda: finish(8))
    send_to(all_gram.at[half(c)], all_gram.at[half(c)], gram_send.at[3], gram_recv.at[3], gx, partner)
    wait_for(all_gram.at[half(1 - c)], gram_recv.at[3])
    for n, (i, j) in enumerate(BLOCKS):
        block = all_gram[128 * n : 128 * (n + 1), :] * (1.0 / (512 * 1024))
        gram_x[128 * i : 128 * (i + 1), 128 * j : 128 * (j + 1)] = block
        if i != j:
            gram_x[128 * j : 128 * (j + 1), 128 * i : 128 * (i + 1)] = block.T

    def normaliser(product):
        return inverse_factor(row_gram(product))

    def iterate(step, product):
        ahead = dot_exact(product, gram_x[...], NN)
        return dot_six(normaliser(product), ahead)

    product = dot_exact(start[...].T, gram_x[...], NN)
    product = lax.fori_loop(0, ITERS - 1, iterate, product)
    rows = dot_six(normaliser(product), product)
    basis[...] = rows.T

    b_high, b_low = split(rows)
    for r in range(ROUNDS):
        h, l = high[r], low[r]
        part = dot(b_high, h, NN) + (dot(b_high, l, NN) + dot(b_low, h, NN))
        h, l = split(part)
        for n, piece in enumerate((h, l, h)):
            core[512 * n + RANK * r : 512 * n + RANK * (r + 1), :] = piece
        h, l = split(part.T)
        for n, piece in enumerate((h, h, l)):
            core_t[:, 512 * n + RANK * r : 512 * n + RANK * (r + 1)] = piece

    def columns_of(parity, n):
        pair = [core[:, pl.ds(pl.multiple_of((2 * j + parity) * 128, 128), 128)] for j in (2 * n, 2 * n + 1)]
        return dot(core_t[...], jnp.concatenate(pair, axis=1), NN)

    for n in range(2):
        value = columns_of(1 - c, n)
        for j in range(2):
            give[2 * n + j] = value[:, 128 * j : 128 * (j + 1)].reshape(16, 64, 128)
        blocks = pl.ds(2 * n, 2)
        send_to(give.at[blocks], pair_y.at[blocks], pair_send.at[n], pair_recv.at[n], gx, partner)
    for n in range(2):
        value = columns_of(c, n)
        wait_for(pair_y.at[pl.ds(2 * n, 2)], pair_recv.at[n])
        for j in range(2):
            block = value[:, 128 * j : 128 * (j + 1)].reshape(16, 64, 128)
            keep[2 * n + j] = block + pair_y[2 * n + j]

    to_gx, to_x = routes()
    plane = [to_gx[i][(a + i) % 4] for a in range(4) for i in range(4)][1:]

    first, second = pl.ds(0, 32), pl.ds(32, 32)
    for n, at in enumerate(plane):
        send_to(keep.at[:, at, second], plane_y.at[gx], y_send.at[0], y_recv.at[0], at, yz)
        if n % 5 == 0:
            to = to_x[1 + n // 5]
            send_to(keep.at[to, :, first], line_y.at[x], y_send.at[1], y_recv.at[1], gx, 2 * to + c)
    plane_y[gx] = keep[:, gx, 32:, :]
    line_y[x] = keep[x, :, :32, :]
    wait_for(line_y.at[pl.ds(0, 3)], y_recv.at[1])
    line_sum[...] = jnp.sum(line_y[...], axis=0)
    for at in plane:
        send_to(line_sum.at[at], upper_y.at[gx], y_send.at[2], y_recv.at[2], at, yz)
    wait_for(plane_y.at[pl.ds(0, 15)], y_recv.at[0])
    plane_sum[...] = jnp.sum(plane_y[...], axis=0)
    for at in to_x[1:]:
        send_to(plane_sum.at[at], lower_y.at[x], y_send.at[3], y_recv.at[3], gx, 2 * at + c)
    upper_y[gx] = line_sum[gx]
    lower_y[x] = plane_sum[x]
    wait_for(upper_y.at[pl.ds(0, 15)], y_recv.at[2])
    wait_for(lower_y.at[pl.ds(0, 3)], y_recv.at[3])
    gram_y[0:32, :] = jnp.sum(upper_y[...], axis=0) * (1.0 / 65536)
    gram_y[32:64, :] = jnp.sum(lower_y[...], axis=0) * (1.0 / 65536)

    for r in range(ROUNDS):
        wait_for(landed.at[r, pl.ds(0, 127 * 32)], field_send.at[r])
    wait_for(pair_gram, gram_send.at[0])
    pl.when(wide)(lambda: wait_for(own_gram.at[pl.ds(0, 15 * 16 + 48 * 8)], gram_send.at[1]))
    pl.when(jnp.logical_not(wide))(lambda: wait_for(own_gram.at[pl.ds(0, 16 * 16 + 47 * 8)], gram_send.at[1]))
    pl.when(wide)(lambda: wait_for(parts_gram.at[pl.ds(0, 63)], gram_send.at[2]))
    pl.when(jnp.logical_not(wide))(lambda: wait_for(parts_gram.at[pl.ds(0, 63), pl.ds(0, 8)], gram_send.at[2]))
    wait_for(all_gram.at[half(c)], gram_send.at[3])
    for n in range(2):
        wait_for(give.at[pl.ds(2 * n, 2)], pair_send.at[n])
    wait_for(plane_y.at[pl.ds(0, 15)], y_send.at[0])
    wait_for(line_y.at[pl.ds(0, 3)], y_send.at[1])
    wait_for(upper_y.at[pl.ds(0, 15)], y_send.at[2])
    wait_for(lower_y.at[pl.ds(0, 3)], y_send.at[3])


def deliver(basis, piece, basis_out, piece_out):
    basis_out[...] = basis[...]
    piece_out[...] = piece[...]


def on_device(field, start):
    vmem = pl.BlockSpec(memory_space=pltpu.VMEM)
    basis, piece = pl.pallas_call(
        kernel,
        out_shape=(
            jax.ShapeDtypeStruct((512, RANK), F32),
            jax.ShapeDtypeStruct((64, 128), F32),
        ),
        in_specs=[pl.BlockSpec(memory_space=pl.ANY), vmem],
        out_specs=(vmem, vmem),
        scratch_shapes=[
            pltpu.VMEM((ROUNDS, 4096, 128), F32),
            pltpu.VMEM((ROUNDS, 512, 1024), BF16),
            pltpu.VMEM((ROUNDS, 512, 1024), BF16),
            pltpu.VMEM((512, 256), F32),
            pltpu.VMEM((256, 256), F32),
            pltpu.VMEM((1280, 128), F32),
            pltpu.VMEM((640, 128), F32),
            pltpu.VMEM((640, 128), F32),
            pltpu.VMEM((64, 16, 128), F32),
            pltpu.VMEM((1280, 128), F32),
            pltpu.VMEM((512, 512), F32),
            pltpu.VMEM((1536, 1024), BF16),
            pltpu.VMEM((1024, 1536), BF16),
            pltpu.VMEM((4, 16, 64, 128), F32),
            pltpu.VMEM((4, 16, 64, 128), F32),
            pltpu.VMEM((4, 16, 64, 128), F32),
            pltpu.VMEM((16, 4, 32, 128), F32),
            pltpu.VMEM((4, 16, 32, 128), F32),
            pltpu.VMEM((16, 32, 128), F32),
            pltpu.VMEM((4, 32, 128), F32),
            pltpu.VMEM((16, 32, 128), F32),
            pltpu.VMEM((4, 32, 128), F32),
            pltpu.SemaphoreType.DMA((ROUNDS,)),
            pltpu.SemaphoreType.DMA((ROUNDS,)),
            pltpu.SemaphoreType.DMA((4,)),
            pltpu.SemaphoreType.DMA((4,)),
            pltpu.SemaphoreType.DMA((2,)),
            pltpu.SemaphoreType.DMA((2,)),
            pltpu.SemaphoreType.DMA((4,)),
            pltpu.SemaphoreType.DMA((4,)),
        ],
        compiler_params=pltpu.CompilerParams(
            collective_id=0, has_side_effects=True, vmem_limit_bytes=56 << 20
        ),
    )(field, start)
    basis, piece = pl.pallas_call(
        deliver,
        out_shape=(
            jax.ShapeDtypeStruct((512, RANK), F32),
            jax.ShapeDtypeStruct((64, 128), F32),
        ),
        in_specs=[vmem, vmem],
        out_specs=(vmem, vmem),
    )(basis, piece)
    return basis, piece.T


def solution(mesh):
    placed = (P("gx", None, "yz"), P())
    return jax.shard_map(
        on_device, mesh=mesh, in_specs=placed, out_specs=(P(), P("yz", "gx")), check_vma=False
    )
```

```python
import functools

import jax
import jax.numpy as jnp
from jax import lax
from jax.experimental import pallas as pl
from jax.experimental.pallas import tpu as pltpu
from jax.sharding import PartitionSpec as P

ITERS = 4
ROUNDS = 4
RANK = 128
STRIP = 32
PANEL = 16
F32 = jnp.float32
BF16 = jnp.bfloat16
MESH = pl.DeviceIdType.MESH
NN = (((1,), (0,)), ((), ()))
NT = (((1,), (1,)), ((), ()))
TN = (((0,), (0,)), ((), ()))
BLOCKS = [(0, 0), (1, 0), (2, 0), (3, 0), (1, 1), (2, 1), (3, 1), (2, 2), (3, 2), (3, 3)]


def dot(left, right, dims, precision=None):
    return lax.dot_general(left, right, dims, precision=precision, preferred_element_type=F32)


def dot_exact(left, right, dims):
    return dot(left, right, dims, lax.Precision.HIGHEST)


def split(value):
    high = value.astype(BF16)
    return high, (value - high.astype(F32)).astype(BF16)


def split3(value):
    high = value.astype(BF16)
    rest = value - high.astype(F32)
    return (high,) + split(rest)


def stacked(value, order, axis):
    parts = split3(value)
    return jnp.concatenate([parts[n] for n in order], axis=axis)


def dot_six(left, right):
    return dot(stacked(left, (0, 0, 1, 0, 1, 2), 1), stacked(right, (0, 1, 0, 2, 1, 0), 0), NN)


def row_gram(value):
    high, middle, low = split3(value)
    mixed = dot(high, middle, NT) + dot(high, low, NT)
    both = jnp.concatenate([high, middle], axis=1)
    return dot(both, both, NT) + (mixed + mixed.T)


def position():
    gx, yz = lax.axis_index("gx"), lax.axis_index("yz")
    return gx, yz, gx // 4, gx % 4, yz // 2, yz % 2


def routes():
    gx, yz, z, y, x, c = position()
    sign = 1 + 2 * c
    to_z, to_y, to_x = ([(at + sign * i) % 4 for i in range(4)] for at in (z, y, x))
    return [[to_z[i] * 4 + to_y[j] for j in range(4)] for i in range(4)], to_x


CHIP_STEPS = [(i, (a + i) % 4, (b + i) % 4) for b in range(4) for a in range(4) for i in range(4)]


def each_other_device(action):
    to_gx, to_x = routes()
    c = lax.axis_index("yz") % 2
    to_x = [jnp.where(c == 0, to_x[i], to_x[(i + 2) % 4]) for i in range(4)]
    to_yz = [[2 * at + c for at in to_x], [2 * at + 1 - c for at in to_x]]
    for group in range(16):
        for flip in range(2):
            for i, j, k in CHIP_STEPS[4 * group : 4 * group + 4]:
                act = functools.partial(action, to_gx[i][j], to_yz[flip][k])
                if (i, j, k % 2, flip) == (0, 0, 0, 0):
                    pl.when(c != k // 2)(act)
                else:
                    act()


def each_other_chip(action):
    to_gx, to_x = routes()
    c = lax.axis_index("yz") % 2
    for i, j, k in CHIP_STEPS[1:]:
        action((i, j, k), to_gx[i][j], to_x[k], to_x[k] * 2 + c)


def meet_all():
    barrier = pltpu.get_barrier_semaphore()
    each_other_device(
        lambda to_gx, to_yz: pl.semaphore_signal(
            barrier, inc=1, device_id=(to_gx, to_yz), device_id_type=MESH
        )
    )
    pl.semaphore_wait(barrier, 127)


def send_to(src, dst, send_sem, recv_sem, to_gx, to_yz):
    pltpu.make_async_remote_copy(
        src_ref=src,
        dst_ref=dst,
        send_sem=send_sem,
        recv_sem=recv_sem,
        device_id=(to_gx, to_yz),
        device_id_type=MESH,
    ).start()


def wait_for(ref, sem):
    pltpu.make_async_copy(ref, ref, sem).wait()


def inverse_factor(cross):
    n = RANK
    row = lax.broadcasted_iota(jnp.int32, (n, n), 0)
    col = lax.broadcasted_iota(jnp.int32, (n, n), 1)
    eye = row == col
    diagonal = jnp.where(eye, cross, 0.0)
    scale_row = lax.rsqrt(jnp.sum(diagonal, axis=0, keepdims=True))
    scale_col = lax.rsqrt(jnp.sum(diagonal, axis=1, keepdims=True))
    a = cross * scale_row * scale_col
    e = jnp.where(eye, 1.0, 0.0)
    local = lax.broadcasted_iota(jnp.int32, (STRIP, n), 0)
    done = []
    for strip in range(n // STRIP):
        ra = a[STRIP * strip : STRIP * (strip + 1)]
        re = e[STRIP * strip : STRIP * (strip + 1)]
        alpha = jnp.zeros((STRIP, n), F32)
        beta = jnp.zeros((STRIP, n), F32)
        for panel in range(STRIP // PANEL):
            base = STRIP * strip + PANEL * panel
            c = [jnp.broadcast_to(ra[:, base + j : base + j + 1], (STRIP, n)) for j in range(PANEL)]
            for pair in range(PANEL // 2):
                k = PANEL * panel + 2 * pair
                c0, c1 = c[2 * pair], c[2 * pair + 1]
                p00, p01, p11 = c0[k : k + 1], c1[k : k + 1], c1[k + 1 : k + 2]
                det = p00 * p11 - p01 * p01
                inv = pltpu.reciprocal(det, approx=True)
                below = local > k + 1
                n0 = jnp.where(below, c0 * p11 - c1 * p01, 0.0)
                n1 = jnp.where(below, c1 * p00 - c0 * p01, 0.0)
                m0, m1 = n0 * inv, n1 * inv
                for j in range(2 * pair + 2, min(2 * pair + 4, PANEL)):
                    c[j] = c[j] - (n0 * c[j][k : k + 1] + n1 * c[j][k + 1 : k + 2]) * inv
                for j in range(2 * pair + 4, PANEL):
                    c[j] = c[j] - m0 * c[j][k : k + 1] - m1 * c[j][k + 1 : k + 2]
                if k + 2 < STRIP:
                    ra = ra - m0 * ra[k : k + 1] - m1 * ra[k + 1 : k + 2]
                    re = re - m0 * re[k : k + 1] - m1 * re[k + 1 : k + 2]
                s0 = lax.rsqrt(p00)
                s1 = lax.rsqrt(det * (s0 * s0))
                alpha = jnp.where(local == k, s0, jnp.where(local == k + 1, s1, alpha))
                beta = jnp.where(local == k + 1, p01 * (s0 * s0), beta)
        ua = alpha * (ra - beta * pltpu.roll(ra, 1, 0))
        ue = alpha * (re - beta * pltpu.roll(re, 1, 0))
        done.append(ue)
        if strip + 1 < n // STRIP:
            left = stacked(ua, (0, 0, 1, 0, 1, 2), 0)
            right = stacked(jnp.concatenate([ua, ue], axis=1), (0, 1, 0, 2, 1, 0), 0)
            update = dot(left, right, TN)
            a = a - update[:, :n]
            e = e - update[:, n:]
    return jnp.concatenate(done, axis=0) * scale_row


def kernel(
    field, start, basis, gram_y,
    landed, high, low, left_half, right_half,
    own_gram, pair_gram, sum_gram, parts_gram, all_gram, gram_x,
    core, core_t, give, keep, pair_y,
    plane_y, line_y, line_sum, plane_sum, upper_y, lower_y,
    field_send, field_recv, gram_send, gram_recv, pair_send, pair_recv, y_send, y_recv,
):
    gx, yz, z, y, x, c = position()
    chip = gx * 4 + x
    meet_all()

    own = pl.ds(pl.multiple_of(yz * 512 + gx * 32, 32), 32)

    def exchange(r, carry):
        pltpu.make_async_copy(
            field.at[:, (gx * 8 + yz) * ROUNDS + r], landed.at[r, own], field_recv.at[r]
        ).start()
        each_other_device(
            lambda to_gx, to_yz: send_to(
                field.at[:, (to_gx * 8 + to_yz) * ROUNDS + r],
                landed.at[r, own],
                field_send.at[r],
                field_recv.at[r],
                to_gx,
                to_yz,
            )
        )
        return carry

    lax.fori_loop(0, ROUNDS, exchange, 0)

    for r in range(ROUNDS):
        wait_for(landed.at[r], field_recv.at[r])
        for j in range(8):
            h, l = split(landed[r, 512 * j : 512 * (j + 1), :])
            high[r, :, 128 * j : 128 * (j + 1)] = h
            low[r, :, 128 * j : 128 * (j + 1)] = l
        h, l = high[r], low[r]
        left = jnp.concatenate([h, h, l], axis=1)
        right = jnp.concatenate([h, l, h], axis=1)
        if r == 0:
            left_half[...] = dot(left, right[:256], NT)
            right_half[...] = dot(left[256:], right[256:], NT)
        else:
            left_half[...] += dot(left, right[:256], NT)
            right_half[...] += dot(left[256:], right[256:], NT)
    for n, (i, j) in enumerate(BLOCKS):
        if j < 2:
            block = left_half[128 * i : 128 * (i + 1), 128 * j : 128 * (j + 1)]
        else:
            block = right_half[128 * (i - 2) : 128 * (i - 1), 128 * (j - 2) : 128 * (j - 1)]
        own_gram[128 * n : 128 * (n + 1), :] = block

    def half(of):
        return pl.ds(pl.multiple_of(of * 640, 128), 640)

    def rows_of(at, place, size):
        start = at * 40 + jnp.where(place == 0, 0, 8 + 8 * place)
        return pl.ds(pl.multiple_of(start, 8), size)

    place = (x + 8 - z - y) % 4
    wide = place == 0
    partner = x * 2 + 1 - c
    send_to(own_gram.at[half(1 - c)], pair_gram, gram_send.at[0], gram_recv.at[0], gx, partner)
    wait_for(pair_gram, gram_recv.at[0])
    sum_gram[...] = own_gram[half(c), :] + pair_gram[...]
    places = [(place + (1 + 2 * c) * n) % 4 for n in range(4)]

    def scatter(steps, to_gx, to_x, to_yz):
        to_place = places[(steps[2] - steps[0] - steps[1]) % 4]

        def part(size):
            send_to(
                sum_gram.at[rows_of(to_gx, to_place, size)], parts_gram.at[chip, pl.ds(0, size)],
                gram_send.at[1], gram_recv.at[1], to_gx, to_yz,
            )

        pl.when(to_place == 0)(lambda: part(16))
        pl.when(to_place != 0)(lambda: part(8))

    each_other_chip(scatter)

    def finish(size):
        mine = rows_of(gx, place, size)
        parts_gram[chip, 0:size] = sum_gram[mine, :]
        wait_for(parts_gram.at[pl.ds(0, 63), pl.ds(0, size)], gram_recv.at[1])
        piece = pl.ds(pl.multiple_of(c * 640 + mine.start, 8), size)
        all_gram[piece, :] = jnp.sum(parts_gram[:, 0:size], axis=0)
        each_other_chip(
            lambda steps, to_gx, to_x, to_yz: send_to(
                all_gram.at[piece], all_gram.at[piece], gram_send.at[2], gram_recv.at[2], to_gx, to_yz
            )
        )
        wait_for(all_gram.at[pl.ds(0, 640 - size)], gram_recv.at[2])

    pl.when(wide)(lambda: finish(16))
    pl.when(jnp.logical_not(wide))(lambda: finish(8))
    send_to(all_gram.at[half(c)], all_gram.at[half(c)], gram_send.at[3], gram_recv.at[3], gx, partner)
    wait_for(all_gram.at[half(1 - c)], gram_recv.at[3])
    for n, (i, j) in enumerate(BLOCKS):
        block = all_gram[128 * n : 128 * (n + 1), :] * (1.0 / (512 * 1024))
        gram_x[128 * i : 128 * (i + 1), 128 * j : 128 * (j + 1)] = block
        if i != j:
            gram_x[128 * j : 128 * (j + 1), 128 * i : 128 * (i + 1)] = block.T

    def normaliser(product):
        return inverse_factor(row_gram(product))

    def iterate(step, product):
        ahead = dot_exact(product, gram_x[...], NN)
        return dot_six(normaliser(product), ahead)

    product = dot_exact(start[...].T, gram_x[...], NN)
    product = lax.fori_loop(0, ITERS - 1, iterate, product)
    rows = dot_six(normaliser(product), product)
    basis[...] = rows.T

    b_high, b_low = split(rows)
    for r in range(ROUNDS):
        h, l = high[r], low[r]
        part = dot(b_high, h, NN) + (dot(b_high, l, NN) + dot(b_low, h, NN))
        h, l = split(part)
        for n, piece in enumerate((h, l, h)):
            core[512 * n + RANK * r : 512 * n + RANK * (r + 1), :] = piece
        h, l = split(part.T)
        for n, piece in enumerate((h, h, l)):
            core_t[:, 512 * n + RANK * r : 512 * n + RANK * (r + 1)] = piece

    def columns_of(parity, n):
        pair = [core[:, pl.ds(pl.multiple_of((2 * j + parity) * 128, 128), 128)] for j in (2 * n, 2 * n + 1)]
        return dot(core_t[...], jnp.concatenate(pair, axis=1), NN)

    for n in range(2):
        value = columns_of(1 - c, n)
        for j in range(2):
            give[2 * n + j] = value[:, 128 * j : 128 * (j + 1)].reshape(16, 64, 128)
        blocks = pl.ds(2 * n, 2)
        send_to(give.at[blocks], pair_y.at[blocks], pair_send.at[n], pair_recv.at[n], gx, partner)
    for n in range(2):
        value = columns_of(c, n)
        for j in range(2):
            keep[2 * n + j] = value[:, 128 * j : 128 * (j + 1)].reshape(16, 64, 128)
    for n in range(2):
        wait_for(pair_y.at[pl.ds(2 * n, 2)], pair_recv.at[n])
        keep[2 * n : 2 * n + 2] = keep[2 * n : 2 * n + 2] + pair_y[2 * n : 2 * n + 2]

    to_gx, to_x = routes()
    plane = [to_gx[i][(a + i) % 4] for a in range(4) for i in range(4)][1:]

    first, second = pl.ds(0, 32), pl.ds(32, 32)
    for to in to_x[1:]:
        send_to(keep.at[to, :, first], line_y.at[x], y_send.at[1], y_recv.at[1], gx, 2 * to + c)
    for at in plane:
        send_to(keep.at[:, at, second], plane_y.at[gx], y_send.at[0], y_recv.at[0], at, yz)
    plane_y[gx] = keep[:, gx, 32:, :]
    line_y[x] = keep[x, :, :32, :]
    wait_for(line_y.at[pl.ds(0, 3)], y_recv.at[1])
    line_sum[...] = jnp.sum(line_y[...], axis=0)
    for at in plane:
        send_to(line_sum.at[at], upper_y.at[gx], y_send.at[2], y_recv.at[2], at, yz)
    wait_for(plane_y.at[pl.ds(0, 15)], y_recv.at[0])
    plane_sum[...] = jnp.sum(plane_y[...], axis=0)
    for at in to_x[1:]:
        send_to(plane_sum.at[at], lower_y.at[x], y_send.at[3], y_recv.at[3], gx, 2 * at + c)
    upper_y[gx] = line_sum[gx]
    lower_y[x] = plane_sum[x]
    wait_for(upper_y.at[pl.ds(0, 15)], y_recv.at[2])
    wait_for(lower_y.at[pl.ds(0, 3)], y_recv.at[3])
    gram_y[0:32, :] = jnp.sum(upper_y[...], axis=0) * (1.0 / 65536)
    gram_y[32:64, :] = jnp.sum(lower_y[...], axis=0) * (1.0 / 65536)

    for r in range(ROUNDS):
        wait_for(landed.at[r, pl.ds(0, 127 * 32)], field_send.at[r])
    wait_for(pair_gram, gram_send.at[0])
    pl.when(wide)(lambda: wait_for(own_gram.at[pl.ds(0, 15 * 16 + 48 * 8)], gram_send.at[1]))
    pl.when(jnp.logical_not(wide))(lambda: wait_for(own_gram.at[pl.ds(0, 16 * 16 + 47 * 8)], gram_send.at[1]))
    pl.when(wide)(lambda: wait_for(parts_gram.at[pl.ds(0, 63)], gram_send.at[2]))
    pl.when(jnp.logical_not(wide))(lambda: wait_for(parts_gram.at[pl.ds(0, 63), pl.ds(0, 8)], gram_send.at[2]))
    wait_for(all_gram.at[half(c)], gram_send.at[3])
    for n in range(2):
        wait_for(give.at[pl.ds(2 * n, 2)], pair_send.at[n])
    wait_for(plane_y.at[pl.ds(0, 15)], y_send.at[0])
    wait_for(line_y.at[pl.ds(0, 3)], y_send.at[1])
    wait_for(upper_y.at[pl.ds(0, 15)], y_send.at[2])
    wait_for(lower_y.at[pl.ds(0, 3)], y_send.at[3])


def deliver(basis, piece, basis_out, piece_out):
    basis_out[...] = basis[...]
    piece_out[...] = piece[...]


def on_device(field, start):
    vmem = pl.BlockSpec(memory_space=pltpu.VMEM)
    basis, piece = pl.pallas_call(
        kernel,
        out_shape=(
            jax.ShapeDtypeStruct((512, RANK), F32),
            jax.ShapeDtypeStruct((64, 128), F32),
        ),
        in_specs=[pl.BlockSpec(memory_space=pl.ANY), vmem],
        out_specs=(vmem, vmem),
        scratch_shapes=[
            pltpu.VMEM((ROUNDS, 4096, 128), F32),
            pltpu.VMEM((ROUNDS, 512, 1024), BF16),
            pltpu.VMEM((ROUNDS, 512, 1024), BF16),
            pltpu.VMEM((512, 256), F32),
            pltpu.VMEM((256, 256), F32),
            pltpu.VMEM((1280, 128), F32),
            pltpu.VMEM((640, 128), F32),
            pltpu.VMEM((640, 128), F32),
            pltpu.VMEM((64, 16, 128), F32),
            pltpu.VMEM((1280, 128), F32),
            pltpu.VMEM((512, 512), F32),
            pltpu.VMEM((1536, 1024), BF16),
            pltpu.VMEM((1024, 1536), BF16),
            pltpu.VMEM((4, 16, 64, 128), F32),
            pltpu.VMEM((4, 16, 64, 128), F32),
            pltpu.VMEM((4, 16, 64, 128), F32),
            pltpu.VMEM((16, 4, 32, 128), F32),
            pltpu.VMEM((4, 16, 32, 128), F32),
            pltpu.VMEM((16, 32, 128), F32),
            pltpu.VMEM((4, 32, 128), F32),
            pltpu.VMEM((16, 32, 128), F32),
            pltpu.VMEM((4, 32, 128), F32),
            pltpu.SemaphoreType.DMA((ROUNDS,)),
            pltpu.SemaphoreType.DMA((ROUNDS,)),
            pltpu.SemaphoreType.DMA((4,)),
            pltpu.SemaphoreType.DMA((4,)),
            pltpu.SemaphoreType.DMA((2,)),
            pltpu.SemaphoreType.DMA((2,)),
            pltpu.SemaphoreType.DMA((4,)),
            pltpu.SemaphoreType.DMA((4,)),
        ],
        compiler_params=pltpu.CompilerParams(
            collective_id=0, has_side_effects=True, vmem_limit_bytes=56 << 20
        ),
    )(field, start)
    basis, piece = pl.pallas_call(
        deliver,
        out_shape=(
            jax.ShapeDtypeStruct((512, RANK), F32),
            jax.ShapeDtypeStruct((64, 128), F32),
        ),
        in_specs=[vmem, vmem],
        out_specs=(vmem, vmem),
    )(basis, piece)
    return basis, piece.T


def solution(mesh):
    placed = (P("gx", None, "yz"), P())
    return jax.shard_map(
        on_device, mesh=mesh, in_specs=placed, out_specs=(P(), P("yz", "gx")), check_vma=False
    )
```

```python
import functools

import jax
import jax.numpy as jnp
from jax import lax
from jax.experimental import pallas as pl
from jax.experimental.pallas import tpu as pltpu
from jax.sharding import PartitionSpec as P

ITERS = 4
ROUNDS = 4
RANK = 128
STRIP = 32
PANEL = 16
F32 = jnp.float32
BF16 = jnp.bfloat16
MESH = pl.DeviceIdType.MESH
NN = (((1,), (0,)), ((), ()))
NT = (((1,), (1,)), ((), ()))
TN = (((0,), (0,)), ((), ()))
BLOCKS = [(0, 0), (1, 0), (2, 0), (3, 0), (1, 1), (2, 1), (3, 1), (2, 2), (3, 2), (3, 3)]


def dot(left, right, dims, precision=None):
    return lax.dot_general(left, right, dims, precision=precision, preferred_element_type=F32)


def dot_exact(left, right, dims):
    return dot(left, right, dims, lax.Precision.HIGHEST)


def split(value):
    high = value.astype(BF16)
    return high, (value - high.astype(F32)).astype(BF16)


def split3(value):
    high = value.astype(BF16)
    rest = value - high.astype(F32)
    return (high,) + split(rest)


def stacked(value, order, axis):
    parts = split3(value)
    return jnp.concatenate([parts[n] for n in order], axis=axis)


def dot_six(left, right):
    return dot(stacked(left, (0, 0, 1, 0, 1, 2), 1), stacked(right, (0, 1, 0, 2, 1, 0), 0), NN)


def row_gram(value):
    high, middle, low = split3(value)
    mixed = dot(high, middle, NT) + dot(high, low, NT)
    both = jnp.concatenate([high, middle], axis=1)
    return dot(both, both, NT) + (mixed + mixed.T)


def position():
    gx, yz = lax.axis_index("gx"), lax.axis_index("yz")
    return gx, yz, gx // 4, gx % 4, yz // 2, yz % 2


def routes():
    gx, yz, z, y, x, c = position()
    sign = 1 + 2 * c
    to_z, to_y, to_x = ([(at + sign * i) % 4 for i in range(4)] for at in (z, y, x))
    return [[to_z[i] * 4 + to_y[j] for j in range(4)] for i in range(4)], to_x


CHIP_STEPS = [(i, (a + 3 * i) % 4, (b + i) % 4) for b in range(4) for a in range(4) for i in range(4)]


def each_other_device(action):
    to_gx, to_x = routes()
    c = lax.axis_index("yz") % 2
    to_x = [jnp.where(c == 0, to_x[i], to_x[(i + 2) % 4]) for i in range(4)]
    to_yz = [[2 * at + c for at in to_x], [2 * at + 1 - c for at in to_x]]
    for group in range(16):
        for flip in range(2):
            for i, j, k in CHIP_STEPS[4 * group : 4 * group + 4]:
                act = functools.partial(action, to_gx[i][j], to_yz[flip][k])
                if (i, j, k % 2, flip) == (0, 0, 0, 0):
                    pl.when(c != k // 2)(act)
                else:
                    act()


def each_other_chip(action):
    to_gx, to_x = routes()
    c = lax.axis_index("yz") % 2
    for i, j, k in CHIP_STEPS[1:]:
        action((i, j, k), to_gx[i][j], to_x[k], to_x[k] * 2 + c)


def meet_all():
    barrier = pltpu.get_barrier_semaphore()
    each_other_device(
        lambda to_gx, to_yz: pl.semaphore_signal(
            barrier, inc=1, device_id=(to_gx, to_yz), device_id_type=MESH
        )
    )
    pl.semaphore_wait(barrier, 127)


def send_to(src, dst, send_sem, recv_sem, to_gx, to_yz):
    pltpu.make_async_remote_copy(
        src_ref=src,
        dst_ref=dst,
        send_sem=send_sem,
        recv_sem=recv_sem,
        device_id=(to_gx, to_yz),
        device_id_type=MESH,
    ).start()


def wait_for(ref, sem):
    pltpu.make_async_copy(ref, ref, sem).wait()


def inverse_factor(cross):
    n = RANK
    row = lax.broadcasted_iota(jnp.int32, (n, n), 0)
    col = lax.broadcasted_iota(jnp.int32, (n, n), 1)
    eye = row == col
    diagonal = jnp.where(eye, cross, 0.0)
    scale_row = lax.rsqrt(jnp.sum(diagonal, axis=0, keepdims=True))
    scale_col = lax.rsqrt(jnp.sum(diagonal, axis=1, keepdims=True))
    a = cross * scale_row * scale_col
    e = jnp.where(eye, 1.0, 0.0)
    local = lax.broadcasted_iota(jnp.int32, (STRIP, n), 0)
    done = []
    for strip in range(n // STRIP):
        ra = a[STRIP * strip : STRIP * (strip + 1)]
        re = e[STRIP * strip : STRIP * (strip + 1)]
        alpha = jnp.zeros((STRIP, n), F32)
        beta = jnp.zeros((STRIP, n), F32)
        for panel in range(STRIP // PANEL):
            base = STRIP * strip + PANEL * panel
            c = [jnp.broadcast_to(ra[:, base + j : base + j + 1], (STRIP, n)) for j in range(PANEL)]
            for pair in range(PANEL // 2):
                k = PANEL * panel + 2 * pair
                c0, c1 = c[2 * pair], c[2 * pair + 1]
                p00, p01, p11 = c0[k : k + 1], c1[k : k + 1], c1[k + 1 : k + 2]
                det = p00 * p11 - p01 * p01
                inv = pltpu.reciprocal(det, approx=True)
                below = local > k + 1
                n0 = jnp.where(below, c0 * p11 - c1 * p01, 0.0)
                n1 = jnp.where(below, c1 * p00 - c0 * p01, 0.0)
                m0, m1 = n0 * inv, n1 * inv
                for j in range(2 * pair + 2, min(2 * pair + 4, PANEL)):
                    c[j] = c[j] - (n0 * c[j][k : k + 1] + n1 * c[j][k + 1 : k + 2]) * inv
                for j in range(2 * pair + 4, PANEL):
                    c[j] = c[j] - m0 * c[j][k : k + 1] - m1 * c[j][k + 1 : k + 2]
                if k + 2 < STRIP:
                    ra = ra - m0 * ra[k : k + 1] - m1 * ra[k + 1 : k + 2]
                    re = re - m0 * re[k : k + 1] - m1 * re[k + 1 : k + 2]
                s0 = lax.rsqrt(p00)
                s1 = lax.rsqrt(det * (s0 * s0))
                alpha = jnp.where(local == k, s0, jnp.where(local == k + 1, s1, alpha))
                beta = jnp.where(local == k + 1, p01 * (s0 * s0), beta)
        ua = alpha * (ra - beta * pltpu.roll(ra, 1, 0))
        ue = alpha * (re - beta * pltpu.roll(re, 1, 0))
        done.append(ue)
        if strip + 1 < n // STRIP:
            left = stacked(ua, (0, 0, 1, 0, 1, 2), 0)
            right = stacked(jnp.concatenate([ua, ue], axis=1), (0, 1, 0, 2, 1, 0), 0)
            update = dot(left, right, TN)
            a = a - update[:, :n]
            e = e - update[:, n:]
    return jnp.concatenate(done, axis=0) * scale_row


def kernel(
    field, start, basis, gram_y,
    landed, high, low, left_half, right_half,
    own_gram, pair_gram, sum_gram, parts_gram, all_gram, gram_x,
    core, core_t, give, keep, pair_y,
    plane_y, line_y, line_sum, plane_sum, upper_y, lower_y,
    field_send, field_recv, gram_send, gram_recv, pair_send, pair_recv, y_send, y_recv,
):
    gx, yz, z, y, x, c = position()
    chip = gx * 4 + x
    meet_all()

    own = pl.ds(pl.multiple_of(yz * 512 + gx * 32, 32), 32)

    def exchange(r, carry):
        pltpu.make_async_copy(
            field.at[:, (gx * 8 + yz) * ROUNDS + r], landed.at[r, own], field_recv.at[r]
        ).start()
        each_other_device(
            lambda to_gx, to_yz: send_to(
                field.at[:, (to_gx * 8 + to_yz) * ROUNDS + r],
                landed.at[r, own],
                field_send.at[r],
                field_recv.at[r],
                to_gx,
                to_yz,
            )
        )
        return carry

    lax.fori_loop(0, ROUNDS, exchange, 0)

    for r in range(ROUNDS):
        wait_for(landed.at[r], field_recv.at[r])
        for j in range(8):
            h, l = split(landed[r, 512 * j : 512 * (j + 1), :])
            high[r, :, 128 * j : 128 * (j + 1)] = h
            low[r, :, 128 * j : 128 * (j + 1)] = l
        h, l = high[r], low[r]
        left = jnp.concatenate([h, h, l], axis=1)
        right = jnp.concatenate([h, l, h], axis=1)
        if r == 0:
            left_half[...] = dot(left, right[:256], NT)
            right_half[...] = dot(left[256:], right[256:], NT)
        else:
            left_half[...] += dot(left, right[:256], NT)
            right_half[...] += dot(left[256:], right[256:], NT)
    for n, (i, j) in enumerate(BLOCKS):
        if j < 2:
            block = left_half[128 * i : 128 * (i + 1), 128 * j : 128 * (j + 1)]
        else:
            block = right_half[128 * (i - 2) : 128 * (i - 1), 128 * (j - 2) : 128 * (j - 1)]
        own_gram[128 * n : 128 * (n + 1), :] = block

    def half(of):
        return pl.ds(pl.multiple_of(of * 640, 128), 640)

    def rows_of(at, place, size):
        start = at * 40 + jnp.where(place == 0, 0, 8 + 8 * place)
        return pl.ds(pl.multiple_of(start, 8), size)

    place = (x + 8 - z - y) % 4
    wide = place == 0
    partner = x * 2 + 1 - c
    send_to(own_gram.at[half(1 - c)], pair_gram, gram_send.at[0], gram_recv.at[0], gx, partner)
    wait_for(pair_gram, gram_recv.at[0])
    sum_gram[...] = own_gram[half(c), :] + pair_gram[...]
    places = [(place + (1 + 2 * c) * n) % 4 for n in range(4)]

    def scatter(steps, to_gx, to_x, to_yz):
        to_place = places[(steps[2] - steps[0] - steps[1]) % 4]

        def part(size):
            send_to(
                sum_gram.at[rows_of(to_gx, to_place, size)], parts_gram.at[chip, pl.ds(0, size)],
                gram_send.at[1], gram_recv.at[1], to_gx, to_yz,
            )

        pl.when(to_place == 0)(lambda: part(16))
        pl.when(to_place != 0)(lambda: part(8))

    each_other_chip(scatter)

    def finish(size):
        mine = rows_of(gx, place, size)
        parts_gram[chip, 0:size] = sum_gram[mine, :]
        wait_for(parts_gram.at[pl.ds(0, 63), pl.ds(0, size)], gram_recv.at[1])
        piece = pl.ds(pl.multiple_of(c * 640 + mine.start, 8), size)
        all_gram[piece, :] = jnp.sum(parts_gram[:, 0:size], axis=0)
        each_other_chip(
            lambda steps, to_gx, to_x, to_yz: send_to(
                all_gram.at[piece], all_gram.at[piece], gram_send.at[2], gram_recv.at[2], to_gx, to_yz
            )
        )
        wait_for(all_gram.at[pl.ds(0, 640 - size)], gram_recv.at[2])

    pl.when(wide)(lambda: finish(16))
    pl.when(jnp.logical_not(wide))(lambda: finish(8))
    send_to(all_gram.at[half(c)], all_gram.at[half(c)], gram_send.at[3], gram_recv.at[3], gx, partner)
    wait_for(all_gram.at[half(1 - c)], gram_recv.at[3])
    for n, (i, j) in enumerate(BLOCKS):
        block = all_gram[128 * n : 128 * (n + 1), :] * (1.0 / (512 * 1024))
        gram_x[128 * i : 128 * (i + 1), 128 * j : 128 * (j + 1)] = block
        if i != j:
            gram_x[128 * j : 128 * (j + 1), 128 * i : 128 * (i + 1)] = block.T

    def normaliser(product):
        return inverse_factor(row_gram(product))

    def iterate(step, product):
        ahead = dot_exact(product, gram_x[...], NN)
        return dot_six(normaliser(product), ahead)

    product = dot_exact(start[...].T, gram_x[...], NN)
    product = lax.fori_loop(0, ITERS - 1, iterate, product)
    rows = dot_six(normaliser(product), product)
    basis[...] = rows.T

    b_high, b_low = split(rows)
    for r in range(ROUNDS):
        h, l = high[r], low[r]
        part = dot(b_high, h, NN) + (dot(b_high, l, NN) + dot(b_low, h, NN))
        h, l = split(part)
        for n, piece in enumerate((h, l, h)):
            core[512 * n + RANK * r : 512 * n + RANK * (r + 1), :] = piece
        h, l = split(part.T)
        for n, piece in enumerate((h, h, l)):
            core_t[:, 512 * n + RANK * r : 512 * n + RANK * (r + 1)] = piece

    def columns_of(parity, n):
        pair = [core[:, pl.ds(pl.multiple_of((2 * j + parity) * 128, 128), 128)] for j in (2 * n, 2 * n + 1)]
        return dot(core_t[...], jnp.concatenate(pair, axis=1), NN)

    for n in range(2):
        value = columns_of(1 - c, n)
        for j in range(2):
            give[2 * n + j] = value[:, 128 * j : 128 * (j + 1)].reshape(16, 64, 128)
        blocks = pl.ds(2 * n, 2)
        send_to(give.at[blocks], pair_y.at[blocks], pair_send.at[n], pair_recv.at[n], gx, partner)
    for n in range(2):
        value = columns_of(c, n)
        for j in range(2):
            keep[2 * n + j] = value[:, 128 * j : 128 * (j + 1)].reshape(16, 64, 128)
    for n in range(2):
        wait_for(pair_y.at[pl.ds(2 * n, 2)], pair_recv.at[n])
        keep[2 * n : 2 * n + 2] = keep[2 * n : 2 * n + 2] + pair_y[2 * n : 2 * n + 2]

    to_gx, to_x = routes()
    plane = [to_gx[i][(a + i) % 4] for a in range(4) for i in range(4)][1:]

    first, second = pl.ds(0, 32), pl.ds(32, 32)
    for to in to_x[1:]:
        send_to(keep.at[to, :, first], line_y.at[x], y_send.at[1], y_recv.at[1], gx, 2 * to + c)
    for at in plane:
        send_to(keep.at[:, at, second], plane_y.at[gx], y_send.at[0], y_recv.at[0], at, yz)
    plane_y[gx] = keep[:, gx, 32:, :]
    line_y[x] = keep[x, :, :32, :]
    wait_for(line_y.at[pl.ds(0, 3)], y_recv.at[1])
    line_sum[...] = jnp.sum(line_y[...], axis=0)
    for at in plane:
        send_to(line_sum.at[at], upper_y.at[gx], y_send.at[2], y_recv.at[2], at, yz)
    wait_for(plane_y.at[pl.ds(0, 15)], y_recv.at[0])
    plane_sum[...] = jnp.sum(plane_y[...], axis=0)
    for at in to_x[1:]:
        send_to(plane_sum.at[at], lower_y.at[x], y_send.at[3], y_recv.at[3], gx, 2 * at + c)
    upper_y[gx] = line_sum[gx]
    lower_y[x] = plane_sum[x]
    wait_for(upper_y.at[pl.ds(0, 15)], y_recv.at[2])
    wait_for(lower_y.at[pl.ds(0, 3)], y_recv.at[3])
    gram_y[0:32, :] = jnp.sum(upper_y[...], axis=0) * (1.0 / 65536)
    gram_y[32:64, :] = jnp.sum(lower_y[...], axis=0) * (1.0 / 65536)

    for r in range(ROUNDS):
        wait_for(landed.at[r, pl.ds(0, 127 * 32)], field_send.at[r])
    wait_for(pair_gram, gram_send.at[0])
    pl.when(wide)(lambda: wait_for(own_gram.at[pl.ds(0, 15 * 16 + 48 * 8)], gram_send.at[1]))
    pl.when(jnp.logical_not(wide))(lambda: wait_for(own_gram.at[pl.ds(0, 16 * 16 + 47 * 8)], gram_send.at[1]))
    pl.when(wide)(lambda: wait_for(parts_gram.at[pl.ds(0, 63)], gram_send.at[2]))
    pl.when(jnp.logical_not(wide))(lambda: wait_for(parts_gram.at[pl.ds(0, 63), pl.ds(0, 8)], gram_send.at[2]))
    wait_for(all_gram.at[half(c)], gram_send.at[3])
    for n in range(2):
        wait_for(give.at[pl.ds(2 * n, 2)], pair_send.at[n])
    wait_for(plane_y.at[pl.ds(0, 15)], y_send.at[0])
    wait_for(line_y.at[pl.ds(0, 3)], y_send.at[1])
    wait_for(upper_y.at[pl.ds(0, 15)], y_send.at[2])
    wait_for(lower_y.at[pl.ds(0, 3)], y_send.at[3])


def deliver(basis, piece, basis_out, piece_out):
    basis_out[...] = basis[...]
    piece_out[...] = piece[...]


def on_device(field, start):
    vmem = pl.BlockSpec(memory_space=pltpu.VMEM)
    basis, piece = pl.pallas_call(
        kernel,
        out_shape=(
            jax.ShapeDtypeStruct((512, RANK), F32),
            jax.ShapeDtypeStruct((64, 128), F32),
        ),
        in_specs=[pl.BlockSpec(memory_space=pl.ANY), vmem],
        out_specs=(vmem, vmem),
        scratch_shapes=[
            pltpu.VMEM((ROUNDS, 4096, 128), F32),
            pltpu.VMEM((ROUNDS, 512, 1024), BF16),
            pltpu.VMEM((ROUNDS, 512, 1024), BF16),
            pltpu.VMEM((512, 256), F32),
            pltpu.VMEM((256, 256), F32),
            pltpu.VMEM((1280, 128), F32),
            pltpu.VMEM((640, 128), F32),
            pltpu.VMEM((640, 128), F32),
            pltpu.VMEM((64, 16, 128), F32),
            pltpu.VMEM((1280, 128), F32),
            pltpu.VMEM((512, 512), F32),
            pltpu.VMEM((1536, 1024), BF16),
            pltpu.VMEM((1024, 1536), BF16),
            pltpu.VMEM((4, 16, 64, 128), F32),
            pltpu.VMEM((4, 16, 64, 128), F32),
            pltpu.VMEM((4, 16, 64, 128), F32),
            pltpu.VMEM((16, 4, 32, 128), F32),
            pltpu.VMEM((4, 16, 32, 128), F32),
            pltpu.VMEM((16, 32, 128), F32),
            pltpu.VMEM((4, 32, 128), F32),
            pltpu.VMEM((16, 32, 128), F32),
            pltpu.VMEM((4, 32, 128), F32),
            pltpu.SemaphoreType.DMA((ROUNDS,)),
            pltpu.SemaphoreType.DMA((ROUNDS,)),
            pltpu.SemaphoreType.DMA((4,)),
            pltpu.SemaphoreType.DMA((4,)),
            pltpu.SemaphoreType.DMA((2,)),
            pltpu.SemaphoreType.DMA((2,)),
            pltpu.SemaphoreType.DMA((4,)),
            pltpu.SemaphoreType.DMA((4,)),
        ],
        compiler_params=pltpu.CompilerParams(
            collective_id=0, has_side_effects=True, vmem_limit_bytes=56 << 20
        ),
    )(field, start)
    basis, piece = pl.pallas_call(
        deliver,
        out_shape=(
            jax.ShapeDtypeStruct((512, RANK), F32),
            jax.ShapeDtypeStruct((64, 128), F32),
        ),
        in_specs=[vmem, vmem],
        out_specs=(vmem, vmem),
    )(basis, piece)
    return basis, piece.T


def solution(mesh):
    placed = (P("gx", None, "yz"), P())
    return jax.shard_map(
        on_device, mesh=mesh, in_specs=placed, out_specs=(P(), P("yz", "gx")), check_vma=False
    )
```
